32 devices in a mesh: lat: 4 (over z), lon: 8 (over y, x, core).
Axes of the slice: x: 2, y: 2, z: 4, core: 2. Of those that a mesh axis runs over, the one named last changes fastest.
Arguments:
- adjoint_in: float32 [2, 32, 32, 1024], P(None, None, 'lat', 'lon'), may hold values from -6 to 6
- lat_weights: float32 [2, 4, 32, 1024], P(None, None, 'lat', 'lon'), may hold values from -0.07 to 1, as said below
- lon_weights: float32 [2, 4, 32, 1024], P(None, None, 'lat', 'lon'), may hold values from -0.07 to 1, as said below
- depart_rows: int32 [2, 32, 8], P(None, 'lat', 'lon'), may hold values from 0 to 28, as said below
- depart_blocks: int32 [2, 32, 8], P(None, 'lat', 'lon'), may hold values from 0 to 7, as said below
- vertical_inverse: float32 [2, 32, 32, 32], P(None, 'lat'), may hold values from -0.36 to 1, as said below
Outputs:
- adjoint_out: float32 [2, 32, 32, 1024], P(None, None, 'lat', 'lon')
The draws below stay inside these ranges and needn't reach their ends.
Inputs may be any that keep to these rules, and one draw needn't show every extreme that they name: `lat_weights`: interpolation weights of the nodes -1, 0, 1, 2 for a fraction of 0 to 1. `lon_weights`: interpolation weights of the nodes -1, 0, 1, 2 for a fraction of 0 to 1. depart_rows[s, i, b] lies between max(0, i - 3) and min(i + 1, 28). depart_blocks[s, i, b] equals (b + d) mod 8 for some d with |d| <= 2; d = 2 or -2 occurs in every draw. `vertical_inverse`: diagonal entries are 1; entries off the diagonal are independent, spread about 0.09, within -0.36 to 0.36.
All inputs are finite; a program needn't handle non-finite values.
Results may differ from the reference program's by a relative error of at most 0.0001.
Values sent between devices are 32-bit elements; how exact they have to be, the bound alone decides.
No kernel may reach another device: no remote copies, remote signals or barrier semaphores. Data moves between devices by JAX's collectives and lax.ppermute only.
A program may use at most 64 MiB of HBM per device.

```python
import jax
import jax.numpy as jnp
from jax import lax

F = 2
K = 32
PTS = 128
R = 2
H = 2
STEPS = 2
NLAT = 32
NLON = 1024
N_LON = 8


def cubic_weights(frac):
    return jnp.stack([-frac * (frac - 1.0) * (frac - 2.0) / 6.0, (frac + 1.0) * (frac - 1.0) * (frac - 2.0) / 2.0, -(frac + 1.0) * frac * (frac - 2.0) / 2.0, (frac + 1.0) * frac * (frac - 1.0) / 6.0], axis=1)


def draw_lat_weights(key, part):
    key = jax.random.fold_in(key, 11)
    frac = jax.random.uniform(key, (STEPS, NLAT, NLON), jnp.float32)
    return cubic_weights(frac)


def draw_lon_weights(key, part):
    key = jax.random.fold_in(key, 12)
    frac = jax.random.uniform(key, (STEPS, NLAT, NLON), jnp.float32)
    return cubic_weights(frac)


def draw_depart_rows(key, part):
    key = jax.random.fold_in(key, 13)
    offset = jax.random.randint(key, (STEPS, NLAT, N_LON), -H, H + 1, jnp.int32)
    row_index = lax.broadcasted_iota(jnp.int32, (STEPS, NLAT, N_LON), 1)
    offset = jnp.where(row_index == 0, -H, jnp.where(row_index == NLAT - 1, H, offset))
    return jnp.clip(row_index + offset - 1, 0, NLAT - 4).astype(jnp.int32)


def draw_depart_blocks(key, part):
    key = jax.random.fold_in(key, 14)
    first_key, second_key = jax.random.split(key)
    shape = (STEPS, NLAT, N_LON)
    wide_offset = jax.random.randint(first_key, shape, -R, R + 1, jnp.int32)
    near_offset = jax.random.randint(second_key, shape, -1, 2, jnp.int32)
    row_index = lax.broadcasted_iota(jnp.int32, shape, 1)
    block_index = lax.broadcasted_iota(jnp.int32, shape, 2)
    polar = (row_index < NLAT // 4) | (row_index >= NLAT - NLAT // 4)
    offset = jnp.where(polar, wide_offset, near_offset)
    offset = jnp.where(row_index == 0, R * (1 - 2 * (block_index % 2)), offset)
    offset = jnp.where(row_index == 1, 0, offset)
    return ((block_index + offset) % N_LON).astype(jnp.int32)


def draw_vertical_inverse(key, part):
    key = jax.random.fold_in(key, 15)
    noise = jnp.clip(jax.random.normal(key, (STEPS, NLAT, K, K), jnp.float32), -4.0, 4.0) * 0.09
    identity = jnp.eye(K, dtype=jnp.float32)[None, None]
    return identity + noise * (1.0 - identity)


def block_levels(key, dims, shards, smallest, largest):
    def one(axis_at, parts):
        draws = jax.random.uniform(jax.random.fold_in(jax.random.fold_in(key, 6), axis_at), (parts,), jnp.float32, smallest / len(shards), largest / len(shards))
        return jnp.repeat(jnp.exp(draws), dims[axis_at] // parts).reshape((-1,) + (1,) * (len(dims) - axis_at - 1))

    gain = one(*shards[0])
    for cut in shards[1:]:
        gain = gain * one(*cut)
    return gain


def scatter_about(rng, shape, deviation, reach, pieces=(), kind=jnp.bfloat16):
    level = block_levels(rng, shape, pieces, -0.22, 0.18) if pieces else 1.0
    array = jax.random.normal(rng, shape, jnp.float32) * deviation * level
    return jnp.minimum(jnp.maximum(array, -reach), reach).astype(kind)


def setup_inputs(seed: int = 0) -> dict:
    key_list = jax.random.split(jax.random.key(seed), 7)
    return {
        "adjoint_in": scatter_about(key_list[0], (F, K, NLAT, NLON), 1.0, 6.0, ((2, 4), (3, 8)), jnp.float32),
        "lat_weights": draw_lat_weights(jax.random.fold_in(key_list[6], 71), 0),
        "lon_weights": draw_lon_weights(jax.random.fold_in(key_list[6], 71), 0),
        "depart_rows": draw_depart_rows(jax.random.fold_in(key_list[6], 71), 0),
        "depart_blocks": draw_depart_blocks(jax.random.fold_in(key_list[6], 71), 0),
        "vertical_inverse": draw_vertical_inverse(jax.random.fold_in(key_list[6], 71), 0),
    }


def scatter_step(carried, lat_w, lon_w, row_table, block_table):
    column = jnp.arange(NLON, dtype=jnp.int32)
    block_of = column // PTS
    within = column % PTS
    base_row = row_table[:, block_of]
    base_col = block_table[:, block_of] * PTS + within[None, :]
    partial_value = jnp.zeros(carried.shape, jnp.float32)
    for m in range(4):
        row_index = (base_row + m).astype(jnp.int32)
        for o in range(4):
            col_index = ((base_col + o - 1) % NLON).astype(jnp.int32)
            term = carried * (lat_w[m] * lon_w[o])[None, None]
            partial_value = partial_value.at[:, :, row_index, col_index].add(term)
    return partial_value


def reference(adjoint_in, lat_weights, lon_weights, depart_rows, depart_blocks, vertical_inverse):
    carried = adjoint_in
    for s in (1, 0):
        partial_value = scatter_step(carried, lat_weights[s], lon_weights[s], depart_rows[s], depart_blocks[s])
        carried = jnp.einsum("imk,fmip->fkip", vertical_inverse[s], partial_value, precision=lax.Precision.HIGHEST)
    return carried
```

```python
import functools

import jax
import jax.numpy as jnp
from jax import lax
from jax.experimental import pallas as pl
from jax.experimental.pallas import tpu as pltpu
from jax.sharding import PartitionSpec as P

R = 2
H = 2
NODES = 4
RING = 8
LOW = H + 1
HIGH = H + 2
VMEM_LIMIT = 48 * 1024 * 1024


def shifted(array, axis, by):
    size = lax.axis_size(axis)
    return lax.ppermute(array, axis, [(i, (i + by) % size) for i in range(size)])


def from_behind(value, axis, steps):
    count = lax.axis_size(axis)
    leading, last = (max(0, -steps), min(count, count - steps))
    return lax.ppermute(value, axis, [(source, source + steps) for source in range(leading, last)])


def spread_local(carried, lat_w, lon_w, row_table, block_table, lat_start, own_block, cycle_size):
    fields, levels, lat_rows, points = carried.shape
    ext_rows = lat_rows + LOW + HIGH
    block_count = 2 * R + 3
    width = block_count * points
    rel_row = row_table - lat_start + LOW
    rel_block = (block_table - own_block + R) % cycle_size
    target = lax.broadcasted_iota(jnp.int32, (ext_rows, 4, lat_rows), 0)
    node = lax.broadcasted_iota(jnp.int32, (ext_rows, 4, lat_rows), 1)
    row_onehot = (target == rel_row[None, None, :] + node).astype(jnp.float32)
    placed_all = []
    for m in range(4):
        lon_row = jnp.zeros((fields, levels, lat_rows, points + 3), jnp.float32)
        for o in range(4):
            term = carried * (lat_w[m] * lon_w[o])[None, None]
            lon_row = lon_row + jnp.pad(term, ((0, 0), (0, 0), (0, 0), (o, 3 - o)))
        placed = jnp.zeros((fields, levels, lat_rows, width), jnp.float32)
        for d in range(2 * R + 1):
            left = (d + 1) * points - 1
            right = width - left - (points + 3)
            selected = (rel_block == d).astype(jnp.float32)[None, None, :, None]
            placed = placed + selected * jnp.pad(lon_row, ((0, 0), (0, 0), (0, 0), (left, right)))
        placed_all.append(placed)
    stacked = jnp.stack(placed_all, axis=2)
    return jnp.einsum("emj,fkmjc->fkec", row_onehot, stacked, precision=lax.Precision.HIGHEST)


def cycle_total(buffer, points):
    block_count = 2 * R + 3
    pieces = [buffer[..., q * points : (q + 1) * points] for q in range(block_count)]
    summed = pieces[R + 1]
    for q in range(block_count):
        if q != R + 1:
            summed = summed + shifted(pieces[q], "lon", q - R - 1)
    return summed


def fold_rims(buffer, lat_rows):
    upper = buffer[:, :, :LOW]
    lower = buffer[:, :, LOW + lat_rows :]
    interior = buffer[:, :, LOW : LOW + lat_rows]
    from_after = from_behind(upper, "lat", -1)
    from_before = from_behind(lower, "lat", 1)
    interior = interior + jnp.pad(from_after, ((0, 0), (0, 0), (lat_rows - LOW, 0), (0, 0)))
    interior = interior + jnp.pad(from_before, ((0, 0), (0, 0), (0, lat_rows - HIGH), (0, 0)))
    return interior


def plain_body(adjoint_in, lat_weights, lon_weights, depart_rows, depart_blocks, vertical_inverse):
    fields, levels, lat_rows, points = adjoint_in.shape
    cycle_size = lax.axis_size("lon")
    own_block = lax.axis_index("lon")
    lat_start = lax.axis_index("lat") * lat_rows
    carried = adjoint_in
    for s in (1, 0):
        partial_value = spread_local(
            carried,
            lat_weights[s],
            lon_weights[s],
            depart_rows[s, :, 0],
            depart_blocks[s, :, 0],
            lat_start,
            own_block,
            cycle_size,
        )
        gathered_rows = cycle_total(partial_value, points)
        interior = fold_rims(gathered_rows, lat_rows)
        carried = jnp.einsum(
            "imk,fmip->fkip", vertical_inverse[s], interior, precision=lax.Precision.HIGHEST
        )
    return carried


def vmem(shape, rank=2):
    return pl.BlockSpec(shape, lambda i: (0,) * rank, memory_space=pltpu.VMEM)


def smem_tile(tile):
    return pl.BlockSpec((8, 128), lambda i: (tile, 0), memory_space=pltpu.SMEM)


def smem_whole(size):
    return pl.BlockSpec((size,), lambda i: (0,), memory_space=pltpu.SMEM)


def call(kernel, out_rows, in_specs, scratch, cost, *args):
    outs = [jax.ShapeDtypeStruct((n, 128), jnp.float32) for n in out_rows]
    return pl.pallas_call(
        kernel,
        grid=(1,),
        out_shape=outs,
        in_specs=in_specs,
        out_specs=[vmem((n, 128)) for n in out_rows],
        scratch_shapes=scratch,
        compiler_params=pltpu.CompilerParams(vmem_limit_bytes=VMEM_LIMIT),
        cost_estimate=pl.CostEstimate(flops=cost, bytes_accessed=cost, transcendentals=0),
    )(*args)


def rolled(value):
    return [pltpu.roll(value, 127, 1), value, pltpu.roll(value, 1, 1), pltpu.roll(value, 2, 1)]


def products(weights):
    turned = rolled(weights)
    return [turned[o][0:4] * turned[o][4 + o : 5 + o] for o in range(NODES)]


def lanes_in(low, high):
    lane = lax.broadcasted_iota(jnp.int32, (4, 128), 1)
    return ((lane >= low) & (lane < high)).astype(jnp.float32)


def main_products(prods):
    return [
        (0, prods[0] * lanes_in(0, 127)),
        (1, prods[1]),
        (2, prods[2] * lanes_in(1, 128)),
        (3, prods[3] * lanes_in(2, 128)),
    ]


def left_products(prods):
    return [(0, prods[0] * lanes_in(127, 128))]


def right_products(prods):
    return [(2, prods[2] * lanes_in(0, 1)), (3, prods[3] * lanes_in(0, 2))]


def add_terms(sources, terms, target, first):
    for m in range(NODES):
        for kk, turned in enumerate(sources):
            total = None
            for o, weight in terms:
                term = turned[o] * weight[m : m + 1]
                total = term if total is None else total + term
            target[first + m, 8 * kk : 8 * kk + 8, :] += total


def assemble(levels, me_ref, adj, lat_w, lon_w, rows, blocks, mx, my, md, w0):
    field = me_ref[0] // 4
    per_row = levels + 8
    lane = lax.broadcasted_iota(jnp.int32, (8, 128), 1)
    table = jnp.zeros((8, 128), jnp.float32)
    for at, value in enumerate((rows[1], blocks[1], rows[0], blocks[0])):
        table = jnp.where(lane == at, value.astype(jnp.float32), table)
    for out in (mx, my, md):
        out[8 * per_row : 8 * per_row + 8, :] = table
    for i in range(8):
        base = i * per_row
        for kk in range(0, levels, 8):
            own = adj[pl.ds((field * levels + kk) * 8 + i, 8, stride=8), :]
            other = adj[pl.ds(((1 - field) * levels + kk) * 8 + i, 8, stride=8), :]
            mx[base + kk : base + kk + 8, :] = own
            my[base + kk : base + kk + 8, :] = other
            md[base + kk : base + kk + 8, :] = other
        for s in (0, 1):
            lat = lat_w[pl.ds(s * 32 + i, 4, stride=8), :]
            lon = lon_w[pl.ds(s * 32 + i, 4, stride=8), :]
            if s == 1:
                for out in (mx, my, md):
                    out[base + levels : base + levels + 4, :] = lat
                    out[base + levels + 4 : base + levels + 8, :] = lon
            else:
                tail = 8 * per_row + 8
                w0[8 * i : 8 * i + 4, :] = lat
                w0[8 * i + 4 : 8 * i + 8, :] = lon
                my[tail + 8 * i : tail + 8 * i + 4, :] = lat
                my[tail + 8 * i + 4 : tail + 8 * i + 8, :] = lon


def first_spread(levels, me_ref, *refs):
    messages, tables = refs[0:8], refs[8:16]
    w0, v1, part, m1, m2, acc = refs[16:]
    per_row = levels + 8
    me, lat_start, even = me_ref[0], me_ref[1], me_ref[2]
    slot = me // 4
    acc[...] = jnp.zeros_like(acc)
    for message, table in zip(messages, tables):

        def row(i, _, message=message, table=table):
            first = table[i, 0].astype(jnp.int32) - lat_start + LOW
            tau = table[i, 1].astype(jnp.int32)
            delta = (tau - me) & 3
            base = pl.multiple_of(i * per_row, 8)

            def work(which, block):
                prods = which(products(message[pl.ds(base + levels, 8), :]))
                sources = [rolled(message[pl.ds(base + kk, 8), :]) for kk in range(0, levels, 8)]
                add_terms(sources, prods, acc, (block // 4) * 15 + first)

            @pl.when(delta == 0)
            def _():
                work(main_products, tau)

            @pl.when(delta == 1)
            def _():
                work(left_products, (tau + 7) & 7)

            @pl.when(delta == 3)
            def _():
                work(right_products, (tau + 1) & 7)

            return 0

        lax.fori_loop(0, 8, row, 0)
    part[...] = acc[...].reshape(part.shape)

    def write(out, part_row, count, row):
        for h in range(2):
            out[h * 8 * levels : (h * 8 + count) * levels, :] = acc[
                h * 15 + part_row : h * 15 + part_row + count
            ].reshape(count * levels, 128)
        at = 16 * levels
        tail = 8 * per_row + 8
        for_y = messages[2][tail + 8 * row : tail + 8 * row + 32, :]
        out[pl.ds(pl.multiple_of(at + slot * 32, 8), 32), :] = w0[8 * row : 8 * row + 32, :]
        out[pl.ds(pl.multiple_of(at + (1 - slot) * 32, 8), 32), :] = for_y
        at += 64
        out[at : at + levels, :] = jnp.concatenate([v1[row + j] for j in range(4)], axis=1)
        at += levels
        out[pl.ds(pl.multiple_of(at + slot * 8, 8), 8), :] = messages[0][8 * per_row : tail, :]
        out[pl.ds(pl.multiple_of(at + (1 - slot) * 8, 8), 8), :] = messages[2][8 * per_row : tail, :]

    @pl.when(even == 1)
    def _():
        write(m1, 7, 8, 4)
        write(m2, 0, 6, 0)

    @pl.when(even == 0)
    def _():
        write(m2, 7, 8, 4)
        write(m1, 0, 6, 0)


def vertical(matrix, column):
    m_high = matrix.astype(jnp.bfloat16)
    m_low = (matrix - m_high.astype(jnp.float32)).astype(jnp.bfloat16)
    c_high = column.astype(jnp.bfloat16)
    c_low = (column - c_high.astype(jnp.float32)).astype(jnp.bfloat16)
    return lax.dot_general(
        jnp.concatenate([m_high, m_low, m_high], axis=0),
        jnp.concatenate([c_high, c_high, c_low], axis=0),
        (((0,), (0,)), ((), ())),
        preferred_element_type=jnp.float32,
    )


def second_spread(levels, me_ref, part, r1, r2, w0, ry, v1, own_tab, y_tab, *refs):
    r1_tabs, r2_tabs, outs, (state, weights, acc) = refs[0:2], refs[2:4], refs[4:12], refs[12:]
    per_row = levels + 8
    me, lat_start, even, at_start, at_end = (me_ref[n] for n in range(5))
    slot = me // 4
    is_even = even == 1

    def before(rows):
        return jnp.where(is_even, r2[rows, :], r1[rows, :])

    def after(rows):
        return jnp.where(is_even, r1[rows, :], r2[rows, :])

    def lines(start, count):
        return slice(start, start + count)

    at_w = 16 * levels
    at_v = at_w + 64
    tail = 8 * per_row + 8
    for h in range(2):
        for j in range(4):
            weights[h * 15 + j] = before(lines(at_w + h * 32 + 8 * j, 8))
        for j in range(3):
            weights[h * 15 + 12 + j] = after(lines(at_w + h * 32 + 8 * j, 8))
    for i in range(8):
        weights[slot * 15 + 4 + i] = w0[lines(8 * i, 8), :]
        weights[(1 - slot) * 15 + 4 + i] = ry[lines(tail + 8 * i, 8), :]
    v_before = before(lines(at_v, levels))
    v_after = after(lines(at_v, levels))
    for n in range(15):
        halves = []
        for h in range(2):
            own = (h * 15 + n - 1) * levels
            there = lines((h * 8 + n) * levels, levels)
            if n == 0:
                value = before(there)
            elif n < 8:
                value = part[lines(own, levels), :] + before(there)
            elif n == 8:
                value = part[lines(own, levels), :]
            else:
                value = part[lines(own, levels), :] + after(lines((h * 8 + n - 9) * levels, levels))
            halves.append(value)
        if n < 4:
            matrix = v_before[:, n * levels : (n + 1) * levels]
        elif n < 12:
            matrix = v1[n - 4]
        else:
            matrix = v_after[:, (n - 12) * levels : (n - 11) * levels]
        result = vertical(matrix, jnp.concatenate(halves, axis=1))
        state[n] = result[:, :128]
        state[15 + n] = result[:, 128:]
    for q in range(8):
        acc[q * 22 + 7 : q * 22 + 15] = jnp.zeros((8, levels, 128), jnp.float32)

    def spread(n, h, row, tau):
        tau = tau.astype(jnp.int32)
        first = row.astype(jnp.int32) - lat_start + 7
        prods = products(weights[h * 15 + n])
        sources = [rolled(state[h * 15 + n, kk : kk + 8, :]) for kk in range(0, levels, 8)]
        add_terms(sources, main_products(prods), acc, (tau ^ me) * 22 + first)
        add_terms(sources, left_products(prods), acc, (((tau + 7) & 7) ^ me) * 22 + first)
        add_terms(sources, right_products(prods), acc, (((tau + 1) & 7) ^ me) * 22 + first)

    for h in range(2):

        def own_row(i, _, h=h):
            mine = slot == h
            spread(i + 4, h, *(jnp.where(mine, own_tab[i, c], y_tab[i, c]) for c in (2, 3)))
            return 0

        def before_row(i, _, h=h):
            spread(i, h, *(jnp.where(is_even, r2_tabs[h][i + 4, c], r1_tabs[h][i + 4, c]) for c in (2, 3)))
            return 0

        def after_row(i, _, h=h):
            spread(i + 12, h, *(jnp.where(is_even, r1_tabs[h][i, c], r2_tabs[h][i, c]) for c in (2, 3)))
            return 0

        lax.fori_loop(0, 8, own_row, 0)

        @pl.when(at_start == 0)
        def _():
            lax.fori_loop(0, 4, before_row, 0)

        @pl.when(at_end == 0)
        def _():
            lax.fori_loop(0, 3, after_row, 0)

    for q in range(8):
        outs[q][...] = acc[q * 22 + 7 : q * 22 + 15].reshape(8 * levels, 128)


def finish(levels, me_ref, own, pair, across, up, diagonal, v0, out):
    field = me_ref[0] // 4
    for i in range(8):
        rows = slice(i * levels, (i + 1) * levels)
        mine = own[rows, :] + pair[rows, :] + across[rows, :]
        other = up[rows, :] + diagonal[rows, :]
        result = vertical(v0[i], jnp.concatenate([mine, other], axis=1))
        for kk in range(0, levels, 8):
            out[pl.ds((field * levels + kk) * 8 + i, 8, stride=8), :] = result[kk : kk + 8, :128]
            out[pl.ds(((1 - field) * levels + kk) * 8 + i, 8, stride=8), :] = result[kk : kk + 8, 128:]


def swap_lon(value, bits):
    return lax.ppermute(value, "lon", [(i, i ^ bits) for i in range(RING)])


def swap_lat(value, odd):
    count = lax.axis_size("lat")
    pairs = [(i, i + 1) for i in range(odd, count - 1, 2)]
    return lax.ppermute(value, "lat", pairs + [(b, a) for a, b in pairs])


def ring_body(adjoint_in, lat_weights, lon_weights, depart_rows, depart_blocks, vertical_inverse):
    fields, levels, lat_rows, points = adjoint_in.shape
    me = lax.axis_index("lon")
    band = lax.axis_index("lat")
    count = lax.axis_size("lat")
    info = jnp.stack([me, band * lat_rows, 1 - band % 2, band == 0, band == count - 1]).astype(jnp.int32)
    per_row = levels + 8
    short = 8 * per_row + 8
    long = short + 64
    table_tile = per_row
    size = adjoint_in.size
    mx, my, md, w0 = call(
        functools.partial(assemble, levels),
        [short, long, short, 64],
        [smem_whole(5), vmem((fields * levels * 8, 128)), vmem((64, 128)), vmem((64, 128))]
        + [vmem((2, 8, 1), 3)] * 2,
        [],
        size,
        info,
        adjoint_in.reshape(-1, points),
        lat_weights.reshape(-1, points),
        lon_weights.reshape(-1, points),
        depart_rows,
        depart_blocks,
    )
    rd, ry, rx = swap_lon(md, 6), swap_lon(my, 4), swap_lon(mx, 2)
    messages = [mx, rx, ry, rd] + [swap_lon(value, 1) for value in (mx, rx, ry, rd)]
    lat_size = 16 * levels + 64 + levels + 16
    part, m1, m2 = call(
        functools.partial(first_spread, levels),
        [30 * levels, lat_size, lat_size],
        [smem_whole(5)]
        + [vmem(value.shape) for value in messages]
        + [smem_tile(table_tile)] * 8
        + [vmem((64, 128)), vmem((8, levels, levels), 3)],
        [pltpu.VMEM((30, levels, 128), jnp.float32)],
        8 * size,
        info,
        *messages,
        *messages,
        w0,
        vertical_inverse[1],
    )
    r1, r2 = swap_lat(m1, 0), swap_lat(m2, 1)
    last = (lat_size - 16) // 8
    pieces = call(
        functools.partial(second_spread, levels),
        [8 * levels] * 8,
        [
            smem_whole(5),
            vmem((30 * levels, 128)),
            vmem((lat_size, 128)),
            vmem((lat_size, 128)),
            vmem((64, 128)),
            vmem((long, 128)),
            vmem((8, levels, levels), 3),
            smem_tile(table_tile),
            smem_tile(table_tile),
        ]
        + [smem_tile(last), smem_tile(last + 1)] * 2,
        [
            pltpu.VMEM((30, levels, 128), jnp.float32),
            pltpu.VMEM((30, 8, 128), jnp.float32),
            pltpu.VMEM((8 * 22, levels, 128), jnp.float32),
        ],
        16 * size,
        info,
        part,
        r1,
        r2,
        w0,
        ry,
        vertical_inverse[1],
        mx,
        ry,
        r1,
        r1,
        r2,
        r2,
    )
    received = {}
    for bits in (6, 4, 2):
        received[bits] = swap_lon(pieces[bits] + swap_lon(pieces[bits + 1], 1), bits)
    pair = swap_lon(pieces[1], 1)
    (out,) = call(
        functools.partial(finish, levels),
        [fields * levels * 8],
        [smem_whole(5)] + [vmem((8 * levels, 128))] * 5 + [vmem((8, levels, levels), 3)],
        [],
        size,
        info,
        pieces[0],
        pair,
        received[2],
        received[4],
        received[6],
        vertical_inverse[0],
    )
    return out.reshape(adjoint_in.shape)


def solution(mesh):
    specs = (
        P(None, None, "lat", "lon"),
        P(None, None, "lat", "lon"),
        P(None, None, "lat", "lon"),
        P(None, "lat", "lon"),
        P(None, "lat", "lon"),
        P(None, "lat", None, None),
    )

    def whole(*args):
        fields, levels, rows, points = args[0].shape
        lat, lon = mesh.shape["lat"], mesh.shape["lon"]
        ring = (fields, lon, rows // lat, points // lon) == (2, RING, 8, 128) and levels % 8 == 0 and levels * 4 == 128
        body = ring_body if ring else plain_body
        return jax.shard_map(body, mesh=mesh, in_specs=specs, out_specs=specs[0], check_vma=False)(*args)

    return whole
```

```python
import functools

import jax
import jax.numpy as jnp
from jax import lax
from jax.experimental import pallas as pl
from jax.experimental.pallas import tpu as pltpu
from jax.sharding import PartitionSpec as P

R = 2
H = 2
NODES = 4
RING = 8
LOW = H + 1
HIGH = H + 2
VMEM_LIMIT = 48 * 1024 * 1024


def shifted(array, axis, by):
    size = lax.axis_size(axis)
    return lax.ppermute(array, axis, [(i, (i + by) % size) for i in range(size)])


def from_behind(value, axis, steps):
    count = lax.axis_size(axis)
    leading, last = (max(0, -steps), min(count, count - steps))
    return lax.ppermute(value, axis, [(source, source + steps) for source in range(leading, last)])


def spread_local(carried, lat_w, lon_w, row_table, block_table, lat_start, own_block, cycle_size):
    fields, levels, lat_rows, points = carried.shape
    ext_rows = lat_rows + LOW + HIGH
    block_count = 2 * R + 3
    width = block_count * points
    rel_row = row_table - lat_start + LOW
    rel_block = (block_table - own_block + R) % cycle_size
    target = lax.broadcasted_iota(jnp.int32, (ext_rows, 4, lat_rows), 0)
    node = lax.broadcasted_iota(jnp.int32, (ext_rows, 4, lat_rows), 1)
    row_onehot = (target == rel_row[None, None, :] + node).astype(jnp.float32)
    placed_all = []
    for m in range(4):
        lon_row = jnp.zeros((fields, levels, lat_rows, points + 3), jnp.float32)
        for o in range(4):
            term = carried * (lat_w[m] * lon_w[o])[None, None]
            lon_row = lon_row + jnp.pad(term, ((0, 0), (0, 0), (0, 0), (o, 3 - o)))
        placed = jnp.zeros((fields, levels, lat_rows, width), jnp.float32)
        for d in range(2 * R + 1):
            left = (d + 1) * points - 1
            right = width - left - (points + 3)
            selected = (rel_block == d).astype(jnp.float32)[None, None, :, None]
            placed = placed + selected * jnp.pad(lon_row, ((0, 0), (0, 0), (0, 0), (left, right)))
        placed_all.append(placed)
    stacked = jnp.stack(placed_all, axis=2)
    return jnp.einsum("emj,fkmjc->fkec", row_onehot, stacked, precision=lax.Precision.HIGHEST)


def cycle_total(buffer, points):
    block_count = 2 * R + 3
    pieces = [buffer[..., q * points : (q + 1) * points] for q in range(block_count)]
    summed = pieces[R + 1]
    for q in range(block_count):
        if q != R + 1:
            summed = summed + shifted(pieces[q], "lon", q - R - 1)
    return summed


def fold_rims(buffer, lat_rows):
    upper = buffer[:, :, :LOW]
    lower = buffer[:, :, LOW + lat_rows :]
    interior = buffer[:, :, LOW : LOW + lat_rows]
    from_after = from_behind(upper, "lat", -1)
    from_before = from_behind(lower, "lat", 1)
    interior = interior + jnp.pad(from_after, ((0, 0), (0, 0), (lat_rows - LOW, 0), (0, 0)))
    interior = interior + jnp.pad(from_before, ((0, 0), (0, 0), (0, lat_rows - HIGH), (0, 0)))
    return interior


def plain_body(adjoint_in, lat_weights, lon_weights, depart_rows, depart_blocks, vertical_inverse):
    fields, levels, lat_rows, points = adjoint_in.shape
    cycle_size = lax.axis_size("lon")
    own_block = lax.axis_index("lon")
    lat_start = lax.axis_index("lat") * lat_rows
    carried = adjoint_in
    for s in (1, 0):
        partial_value = spread_local(
            carried,
            lat_weights[s],
            lon_weights[s],
            depart_rows[s, :, 0],
            depart_blocks[s, :, 0],
            lat_start,
            own_block,
            cycle_size,
        )
        gathered_rows = cycle_total(partial_value, points)
        interior = fold_rims(gathered_rows, lat_rows)
        carried = jnp.einsum(
            "imk,fmip->fkip", vertical_inverse[s], interior, precision=lax.Precision.HIGHEST
        )
    return carried


def vmem(shape, rank=2):
    return pl.BlockSpec(shape, lambda i: (0,) * rank, memory_space=pltpu.VMEM)


def smem_tile(tile):
    return pl.BlockSpec((8, 128), lambda i: (tile, 0), memory_space=pltpu.SMEM)


def smem_whole(size):
    return pl.BlockSpec((size,), lambda i: (0,), memory_space=pltpu.SMEM)


def call(kernel, out_rows, in_specs, scratch, cost, *args):
    outs = [jax.ShapeDtypeStruct((n, 128), jnp.float32) for n in out_rows]
    return pl.pallas_call(
        kernel,
        grid=(1,),
        out_shape=outs,
        in_specs=in_specs,
        out_specs=[vmem((n, 128)) for n in out_rows],
        scratch_shapes=scratch,
        compiler_params=pltpu.CompilerParams(vmem_limit_bytes=VMEM_LIMIT),
        cost_estimate=pl.CostEstimate(flops=cost, bytes_accessed=cost, transcendentals=0),
    )(*args)


def rolled(value):
    return [pltpu.roll(value, 127, 1), value, pltpu.roll(value, 1, 1), pltpu.roll(value, 2, 1)]


def products(weights):
    turned = rolled(weights)
    return [turned[o][0:4] * turned[o][4 + o : 5 + o] for o in range(NODES)]


def lane_masks():
    lane = lax.broadcasted_iota(jnp.int32, (8, 128), 1)
    node = lax.broadcasted_iota(jnp.int32, (8, 128), 0)
    first = jnp.maximum(node - 1, 0)
    stay = (lane >= first) & (lane < jnp.where(node == 0, 127, 128))
    return [value.astype(jnp.float32) for value in (stay, (node == 0) & (lane == 127), (node >= 2) & (lane < first))]


def masked(prods, mask, nodes):
    return [(o, prods[o] * mask[o : o + 1]) for o in nodes]


def add_terms(sources, terms, target, first):
    for m in range(NODES):
        for kk, turned in enumerate(sources):
            total = None
            for o, weight in terms:
                term = turned[o] * weight[m : m + 1]
                total = term if total is None else total + term
            target[first + m, 8 * kk : 8 * kk + 8, :] += total


def assemble(levels, me_ref, adj, lat_w, lon_w, rows, blocks, mx, my, md, w0):
    field = me_ref[0] // 4
    per_row = levels + 8
    lane = lax.broadcasted_iota(jnp.int32, (8, 128), 1)
    table = jnp.zeros((8, 128), jnp.float32)
    for at, value in enumerate((rows[1], blocks[1], rows[0], blocks[0])):
        table = jnp.where(lane == at, value.astype(jnp.float32), table)
    for out in (mx, my, md):
        out[8 * per_row : 8 * per_row + 8, :] = table
    for i in range(8):
        base = i * per_row
        for kk in range(0, levels, 8):
            own = adj[pl.ds((field * levels + kk) * 8 + i, 8, stride=8), :]
            other = adj[pl.ds(((1 - field) * levels + kk) * 8 + i, 8, stride=8), :]
            mx[base + kk : base + kk + 8, :] = own
            my[base + kk : base + kk + 8, :] = other
            md[base + kk : base + kk + 8, :] = other
        for s in (0, 1):
            lat = lat_w[pl.ds(s * 32 + i, 4, stride=8), :]
            lon = lon_w[pl.ds(s * 32 + i, 4, stride=8), :]
            if s == 1:
                for out in (mx, my, md):
                    out[base + levels : base + levels + 4, :] = lat
                    out[base + levels + 4 : base + levels + 8, :] = lon
            else:
                tail = 8 * per_row + 8
                w0[8 * i : 8 * i + 4, :] = lat
                w0[8 * i + 4 : 8 * i + 8, :] = lon
                my[tail + 8 * i : tail + 8 * i + 4, :] = lat
                my[tail + 8 * i + 4 : tail + 8 * i + 8, :] = lon


def first_spread(levels, me_ref, *refs):
    messages, tables = refs[0:8], refs[8:16]
    w0, v1, part, m1, m2, acc, masks = refs[16:]
    per_row = levels + 8
    me, lat_start, even = me_ref[0], me_ref[1], me_ref[2]
    slot = me // 4
    acc[...] = jnp.zeros_like(acc)
    stay, back, on = lane_masks()
    for n, mask in enumerate((stay, back, jnp.zeros_like(stay), on)):
        masks[n] = mask
    for message, table in zip(messages, tables):

        def row(i, _, message=message, table=table):
            first = table[i, 0].astype(jnp.int32) - lat_start + LOW
            tau = table[i, 1].astype(jnp.int32)
            delta = (tau - me) & 3
            block = (tau + jnp.where(delta == 1, 7, jnp.where(delta == 3, 1, 0))) & 7
            base = pl.multiple_of(i * per_row, 8)
            terms = masked(products(message[pl.ds(base + levels, 8), :]), masks[delta], range(NODES))
            sources = [rolled(message[pl.ds(base + kk, 8), :]) for kk in range(0, levels, 8)]
            add_terms(sources, terms, acc, (block // 4) * 15 + first)
            return 0

        lax.fori_loop(0, 8, row, 0, unroll=True)
    part[...] = acc[...].reshape(part.shape)

    def write(out, part_row, count, row):
        for h in range(2):
            out[h * 8 * levels : (h * 8 + count) * levels, :] = acc[
                h * 15 + part_row : h * 15 + part_row + count
            ].reshape(count * levels, 128)
        at = 16 * levels
        tail = 8 * per_row + 8
        for_y = messages[2][tail + 8 * row : tail + 8 * row + 32, :]
        out[pl.ds(pl.multiple_of(at + slot * 32, 8), 32), :] = w0[8 * row : 8 * row + 32, :]
        out[pl.ds(pl.multiple_of(at + (1 - slot) * 32, 8), 32), :] = for_y
        at += 64
        out[at : at + levels, :] = jnp.concatenate([v1[row + j] for j in range(4)], axis=1)
        at += levels
        out[pl.ds(pl.multiple_of(at + slot * 8, 8), 8), :] = messages[0][8 * per_row : tail, :]
        out[pl.ds(pl.multiple_of(at + (1 - slot) * 8, 8), 8), :] = messages[2][8 * per_row : tail, :]

    @pl.when(even == 1)
    def _():
        write(m1, 7, 8, 4)
        write(m2, 0, 6, 0)

    @pl.when(even == 0)
    def _():
        write(m2, 7, 8, 4)
        write(m1, 0, 6, 0)


def vertical(matrix, column):
    m_high = matrix.astype(jnp.bfloat16)
    m_low = (matrix - m_high.astype(jnp.float32)).astype(jnp.bfloat16)
    c_high = column.astype(jnp.bfloat16)
    c_low = (column - c_high.astype(jnp.float32)).astype(jnp.bfloat16)
    return lax.dot_general(
        jnp.concatenate([m_high, m_low, m_high], axis=0),
        jnp.concatenate([c_high, c_high, c_low], axis=0),
        (((0,), (0,)), ((), ())),
        preferred_element_type=jnp.float32,
    )


def second_spread(levels, me_ref, part, r1, r2, w0, ry, v1, own_tab, y_tab, *refs):
    r1_tabs, r2_tabs, outs, (state, weights, acc) = refs[0:2], refs[2:4], refs[4:12], refs[12:]
    per_row = levels + 8
    me, lat_start, even, at_start, at_end = (me_ref[n] for n in range(5))
    slot = me // 4
    is_even = even == 1

    def before(rows):
        return jnp.where(is_even, r2[rows, :], r1[rows, :])

    def after(rows):
        return jnp.where(is_even, r1[rows, :], r2[rows, :])

    def lines(start, count):
        return slice(start, start + count)

    at_w = 16 * levels
    at_v = at_w + 64
    tail = 8 * per_row + 8
    for h in range(2):
        for j in range(4):
            weights[h * 15 + j] = before(lines(at_w + h * 32 + 8 * j, 8))
        for j in range(3):
            weights[h * 15 + 12 + j] = after(lines(at_w + h * 32 + 8 * j, 8))
    for i in range(8):
        weights[slot * 15 + 4 + i] = w0[lines(8 * i, 8), :]
        weights[(1 - slot) * 15 + 4 + i] = ry[lines(tail + 8 * i, 8), :]
    v_before = before(lines(at_v, levels))
    v_after = after(lines(at_v, levels))
    for n in range(15):
        halves = []
        for h in range(2):
            own = (h * 15 + n - 1) * levels
            there = lines((h * 8 + n) * levels, levels)
            if n == 0:
                value = before(there)
            elif n < 8:
                value = part[lines(own, levels), :] + before(there)
            elif n == 8:
                value = part[lines(own, levels), :]
            else:
                value = part[lines(own, levels), :] + after(lines((h * 8 + n - 9) * levels, levels))
            halves.append(value)
        if n < 4:
            matrix = v_before[:, n * levels : (n + 1) * levels]
        elif n < 12:
            matrix = v1[n - 4]
        else:
            matrix = v_after[:, (n - 12) * levels : (n - 11) * levels]
        result = vertical(matrix, jnp.concatenate(halves, axis=1))
        state[n] = result[:, :128]
        state[15 + n] = result[:, 128:]
    for q in range(8):
        acc[q * 22 + 7 : q * 22 + 15] = jnp.zeros((8, levels, 128), jnp.float32)

    stay, back, on = lane_masks()

    def spread(n, h, row, tau):
        tau = tau.astype(jnp.int32)
        first = row.astype(jnp.int32) - lat_start + 7
        prods = products(weights[h * 15 + n])
        sources = [rolled(state[h * 15 + n, kk : kk + 8, :]) for kk in range(0, levels, 8)]
        add_terms(sources, masked(prods, stay, range(NODES)), acc, (tau ^ me) * 22 + first)
        add_terms(sources, masked(prods, back, (0,)), acc, (((tau + 7) & 7) ^ me) * 22 + first)
        add_terms(sources, masked(prods, on, (2, 3)), acc, (((tau + 1) & 7) ^ me) * 22 + first)

    for h in range(2):

        def own_row(i, _, h=h):
            mine = slot == h
            spread(i + 4, h, *(jnp.where(mine, own_tab[i, c], y_tab[i, c]) for c in (2, 3)))
            return 0

        def before_row(i, _, h=h):
            spread(i, h, *(jnp.where(is_even, r2_tabs[h][i + 4, c], r1_tabs[h][i + 4, c]) for c in (2, 3)))
            return 0

        def after_row(i, _, h=h):
            spread(i + 12, h, *(jnp.where(is_even, r1_tabs[h][i, c], r2_tabs[h][i, c]) for c in (2, 3)))
            return 0

        lax.fori_loop(0, 8, own_row, 0, unroll=True)

        @pl.when(at_start == 0)
        def _():
            lax.fori_loop(0, 4, before_row, 0, unroll=True)

        @pl.when(at_end == 0)
        def _():
            lax.fori_loop(0, 3, after_row, 0, unroll=True)

    for q in range(8):
        outs[q][...] = acc[q * 22 + 7 : q * 22 + 15].reshape(8 * levels, 128)


def finish(levels, me_ref, own, pair, across, up, diagonal, v0, out):
    field = me_ref[0] // 4
    for i in range(8):
        rows = slice(i * levels, (i + 1) * levels)
        mine = own[rows, :] + pair[rows, :] + across[rows, :]
        other = up[rows, :] + diagonal[rows, :]
        result = vertical(v0[i], jnp.concatenate([mine, other], axis=1))
        for kk in range(0, levels, 8):
            out[pl.ds((field * levels + kk) * 8 + i, 8, stride=8), :] = result[kk : kk + 8, :128]
            out[pl.ds(((1 - field) * levels + kk) * 8 + i, 8, stride=8), :] = result[kk : kk + 8, 128:]


def swap_lon(value, bits):
    return lax.ppermute(value, "lon", [(i, i ^ bits) for i in range(RING)])


def swap_lat(value, odd):
    count = lax.axis_size("lat")
    pairs = [(i, i + 1) for i in range(odd, count - 1, 2)]
    return lax.ppermute(value, "lat", pairs + [(b, a) for a, b in pairs])


def ring_body(adjoint_in, lat_weights, lon_weights, depart_rows, depart_blocks, vertical_inverse):
    fields, levels, lat_rows, points = adjoint_in.shape
    me = lax.axis_index("lon")
    band = lax.axis_index("lat")
    count = lax.axis_size("lat")
    info = jnp.stack([me, band * lat_rows, 1 - band % 2, band == 0, band == count - 1]).astype(jnp.int32)
    per_row = levels + 8
    short = 8 * per_row + 8
    long = short + 64
    table_tile = per_row
    size = adjoint_in.size
    mx, my, md, w0 = call(
        functools.partial(assemble, levels),
        [short, long, short, 64],
        [smem_whole(5), vmem((fields * levels * 8, 128)), vmem((64, 128)), vmem((64, 128))]
        + [vmem((2, 8, 1), 3)] * 2,
        [],
        size,
        info,
        adjoint_in.reshape(-1, points),
        lat_weights.reshape(-1, points),
        lon_weights.reshape(-1, points),
        depart_rows,
        depart_blocks,
    )
    rd, ry, rx = swap_lon(md, 6), swap_lon(my, 4), swap_lon(mx, 2)
    messages = [mx, rx, ry, rd] + [swap_lon(value, 1) for value in (mx, rx, ry, rd)]
    lat_size = 16 * levels + 64 + levels + 16
    part, m1, m2 = call(
        functools.partial(first_spread, levels),
        [30 * levels, lat_size, lat_size],
        [smem_whole(5)]
        + [vmem(value.shape) for value in messages]
        + [smem_tile(table_tile)] * 8
        + [vmem((64, 128)), vmem((8, levels, levels), 3)],
        [pltpu.VMEM((30, levels, 128), jnp.float32), pltpu.VMEM((4, 8, 128), jnp.float32)],
        8 * size,
        info,
        *messages,
        *messages,
        w0,
        vertical_inverse[1],
    )
    r1, r2 = swap_lat(m1, 0), swap_lat(m2, 1)
    last = (lat_size - 16) // 8
    pieces = call(
        functools.partial(second_spread, levels),
        [8 * levels] * 8,
        [
            smem_whole(5),
            vmem((30 * levels, 128)),
            vmem((lat_size, 128)),
            vmem((lat_size, 128)),
            vmem((64, 128)),
            vmem((long, 128)),
            vmem((8, levels, levels), 3),
            smem_tile(table_tile),
            smem_tile(table_tile),
        ]
        + [smem_tile(last), smem_tile(last + 1)] * 2,
        [
            pltpu.VMEM((30, levels, 128), jnp.float32),
            pltpu.VMEM((30, 8, 128), jnp.float32),
            pltpu.VMEM((8 * 22, levels, 128), jnp.float32),
        ],
        16 * size,
        info,
        part,
        r1,
        r2,
        w0,
        ry,
        vertical_inverse[1],
        mx,
        ry,
        r1,
        r1,
        r2,
        r2,
    )
    received = {}
    for bits in (6, 4, 2):
        received[bits] = swap_lon(pieces[bits] + swap_lon(pieces[bits + 1], 1), bits)
    pair = swap_lon(pieces[1], 1)
    (out,) = call(
        functools.partial(finish, levels),
        [fields * levels * 8],
        [smem_whole(5)] + [vmem((8 * levels, 128))] * 5 + [vmem((8, levels, levels), 3)],
        [],
        size,
        info,
        pieces[0],
        pair,
        received[2],
        received[4],
        received[6],
        vertical_inverse[0],
    )
    return out.reshape(adjoint_in.shape)


def solution(mesh):
    specs = (
        P(None, None, "lat", "lon"),
        P(None, None, "lat", "lon"),
        P(None, None, "lat", "lon"),
        P(None, "lat", "lon"),
        P(None, "lat", "lon"),
        P(None, "lat", None, None),
    )

    def whole(*args):
        fields, levels, rows, points = args[0].shape
        lat, lon = mesh.shape["lat"], mesh.shape["lon"]
        ring = (fields, lon, rows // lat, points // lon) == (2, RING, 8, 128) and levels % 8 == 0 and levels * 4 == 128
        body = ring_body if ring else plain_body
        return jax.shard_map(body, mesh=mesh, in_specs=specs, out_specs=specs[0], check_vma=False)(*args)

    return whole
```

```python
import functools

import jax
import jax.numpy as jnp
from jax import lax
from jax.experimental import pallas as pl
from jax.experimental.pallas import tpu as pltpu
from jax.sharding import PartitionSpec as P

R = 2
H = 2
NODES = 4
RING = 8
LOW = H + 1
HIGH = H + 2
VMEM_LIMIT = 48 * 1024 * 1024


def shifted(array, axis, by):
    size = lax.axis_size(axis)
    return lax.ppermute(array, axis, [(i, (i + by) % size) for i in range(size)])


def from_behind(value, axis, steps):
    count = lax.axis_size(axis)
    leading, last = (max(0, -steps), min(count, count - steps))
    return lax.ppermute(value, axis, [(source, source + steps) for source in range(leading, last)])


def spread_local(carried, lat_w, lon_w, row_table, block_table, lat_start, own_block, cycle_size):
    fields, levels, lat_rows, points = carried.shape
    ext_rows = lat_rows + LOW + HIGH
    block_count = 2 * R + 3
    width = block_count * points
    rel_row = row_table - lat_start + LOW
    rel_block = (block_table - own_block + R) % cycle_size
    target = lax.broadcasted_iota(jnp.int32, (ext_rows, 4, lat_rows), 0)
    node = lax.broadcasted_iota(jnp.int32, (ext_rows, 4, lat_rows), 1)
    row_onehot = (target == rel_row[None, None, :] + node).astype(jnp.float32)
    placed_all = []
    for m in range(4):
        lon_row = jnp.zeros((fields, levels, lat_rows, points + 3), jnp.float32)
        for o in range(4):
            term = carried * (lat_w[m] * lon_w[o])[None, None]
            lon_row = lon_row + jnp.pad(term, ((0, 0), (0, 0), (0, 0), (o, 3 - o)))
        placed = jnp.zeros((fields, levels, lat_rows, width), jnp.float32)
        for d in range(2 * R + 1):
            left = (d + 1) * points - 1
            right = width - left - (points + 3)
            selected = (rel_block == d).astype(jnp.float32)[None, None, :, None]
            placed = placed + selected * jnp.pad(lon_row, ((0, 0), (0, 0), (0, 0), (left, right)))
        placed_all.append(placed)
    stacked = jnp.stack(placed_all, axis=2)
    return jnp.einsum("emj,fkmjc->fkec", row_onehot, stacked, precision=lax.Precision.HIGHEST)


def cycle_total(buffer, points):
    block_count = 2 * R + 3
    pieces = [buffer[..., q * points : (q + 1) * points] for q in range(block_count)]
    summed = pieces[R + 1]
    for q in range(block_count):
        if q != R + 1:
            summed = summed + shifted(pieces[q], "lon", q - R - 1)
    return summed


def fold_rims(buffer, lat_rows):
    upper = buffer[:, :, :LOW]
    lower = buffer[:, :, LOW + lat_rows :]
    interior = buffer[:, :, LOW : LOW + lat_rows]
    from_after = from_behind(upper, "lat", -1)
    from_before = from_behind(lower, "lat", 1)
    interior = interior + jnp.pad(from_after, ((0, 0), (0, 0), (lat_rows - LOW, 0), (0, 0)))
    interior = interior + jnp.pad(from_before, ((0, 0), (0, 0), (0, lat_rows - HIGH), (0, 0)))
    return interior


def plain_body(adjoint_in, lat_weights, lon_weights, depart_rows, depart_blocks, vertical_inverse):
    fields, levels, lat_rows, points = adjoint_in.shape
    cycle_size = lax.axis_size("lon")
    own_block = lax.axis_index("lon")
    lat_start = lax.axis_index("lat") * lat_rows
    carried = adjoint_in
    for s in (1, 0):
        partial_value = spread_local(
            carried,
            lat_weights[s],
            lon_weights[s],
            depart_rows[s, :, 0],
            depart_blocks[s, :, 0],
            lat_start,
            own_block,
            cycle_size,
        )
        gathered_rows = cycle_total(partial_value, points)
        interior = fold_rims(gathered_rows, lat_rows)
        carried = jnp.einsum(
            "imk,fmip->fkip", vertical_inverse[s], interior, precision=lax.Precision.HIGHEST
        )
    return carried


def vmem(shape, rank=2):
    return pl.BlockSpec(shape, lambda i: (0,) * rank, memory_space=pltpu.VMEM)


def smem_tile(tile):
    return pl.BlockSpec((8, 128), lambda i: (tile, 0), memory_space=pltpu.SMEM)


def smem_whole(size):
    return pl.BlockSpec((size,), lambda i: (0,), memory_space=pltpu.SMEM)


def call(kernel, out_rows, in_specs, scratch, cost, *args):
    sizes = [n if isinstance(n, tuple) else (n, jnp.float32) for n in out_rows]
    outs = [jax.ShapeDtypeStruct((n, 128), dtype) for n, dtype in sizes]
    return pl.pallas_call(
        kernel,
        grid=(1,),
        out_shape=outs,
        in_specs=in_specs,
        out_specs=[vmem((n, 128)) for n, _ in sizes],
        scratch_shapes=scratch,
        compiler_params=pltpu.CompilerParams(vmem_limit_bytes=VMEM_LIMIT),
        cost_estimate=pl.CostEstimate(flops=cost, bytes_accessed=cost, transcendentals=0),
    )(*args)


def rolled(value):
    return [pltpu.roll(value, 127, 1), value, pltpu.roll(value, 1, 1), pltpu.roll(value, 2, 1)]


def products(weights):
    turned = rolled(weights)
    return [turned[o][0:4] * turned[o][4 + o : 5 + o] for o in range(NODES)]


def lane_masks():
    lane = lax.broadcasted_iota(jnp.int32, (8, 128), 1)
    node = lax.broadcasted_iota(jnp.int32, (8, 128), 0)
    first = jnp.maximum(node - 1, 0)
    stay = (lane >= first) & (lane < jnp.where(node == 0, 127, 128))
    return [value.astype(jnp.float32) for value in (stay, (node == 0) & (lane == 127), (node >= 2) & (lane < first))]


def masked(prods, mask, nodes):
    return [(o, prods[o] * mask[o : o + 1]) for o in nodes]


def add_terms(sources, terms, target, first):
    for m in range(NODES):
        for kk, turned in enumerate(sources):
            total = None
            for o, weight in terms:
                term = turned[o] * weight[m : m + 1]
                total = term if total is None else total + term
            target[first + m, 8 * kk : 8 * kk + 8, :] += total


def assemble(levels, rows, blocks, adj, lat_w, lon_w, v, own, other, e1, e2, *scratch):
    tables, lat0, lon0, v1, sems = scratch
    field, even = lax.axis_index("lon") // 4, 1 - lax.axis_index("lat") % 2
    per_field = 8 * levels
    sem = iter(range(16))

    def copy(source, target):
        return pltpu.make_async_copy(source, target, sems.at[next(sem)])

    small = [copy(rows, tables.at[0]), copy(blocks, tables.at[1])]
    small += [copy(lat_w.at[pl.ds(0, 32)], lat0), copy(lon_w.at[pl.ds(0, 32)], lon0), copy(v.at[1], v1)]
    large = []
    for out, which in ((own, field), (other, 1 - field)):
        large.append(copy(adj.at[pl.ds(pl.multiple_of(which * per_field, per_field), per_field)], out.at[pl.ds(0, per_field)]))
        large.append(copy(lat_w.at[pl.ds(32, 32)], out.at[pl.ds(per_field, 32)]))
        large.append(copy(lon_w.at[pl.ds(32, 32)], out.at[pl.ds(per_field + 32, 32)]))
    for each in small + large:
        each.start()
    for each in small:
        each.wait()
    table = jnp.concatenate([tables[0], tables[1], tables[0], tables[1]], axis=0).astype(jnp.float32)
    for out, first in ((own, per_field + 64), (other, per_field + 64), (e1, 32 + levels), (e2, 32 + levels)):
        out[first : first + 8, 0:8] = table
    low = jnp.concatenate([v1[j] for j in range(4)], axis=1)
    high = jnp.concatenate([v1[j + 4] for j in range(4)], axis=1)
    for out, takes_high in ((e1, even == 1), (e2, even == 0)):
        first = jnp.where(takes_high, 4, 0)
        for i in range(4):
            out[8 * i : 8 * i + 4, :] = lat0[pl.ds(first + i, 4, stride=8), :]
            out[8 * i + 4 : 8 * i + 8, :] = lon0[pl.ds(first + i, 4, stride=8), :]
        out[32 : 32 + levels, :] = jnp.where(takes_high, high, low)
    for each in large:
        each.wait()


def rim_data(levels, me_ref, own_tile, lat_w, lon_w, e1, e2, v, after_this, pack, matrices1, matrices0):
    even = me_ref[2] == 1
    for i in range(8):
        pack[32 + 8 * i : 36 + 8 * i, :] = lat_w[pl.ds(i, 4, stride=8), :]
        pack[36 + 8 * i : 40 + 8 * i, :] = lon_w[pl.ds(i, 4, stride=8), :]
    pack[0:32, :] = jnp.where(even, e2[0:32, :], e1[0:32, :])
    pack[96:120, :] = jnp.where(even, e1[0:24, :], e2[0:24, :])
    tab = slice(32 + levels, 40 + levels)
    before = pltpu.roll(jnp.where(even, e2[tab, :], e1[tab, :]), 124, 1)
    after = pltpu.roll(jnp.where(even, e1[tab, :], e2[tab, :]), 12, 1)
    lane = lax.broadcasted_iota(jnp.int32, (8, 128), 1)
    pack[120:128, :] = jnp.where(lane < 4, before, jnp.where(lane < 12, pltpu.roll(own_tile[...], 4, 1), after))

    def turned(four):
        value = four.T
        high = value.astype(jnp.bfloat16).astype(jnp.float32)
        low = value - high
        return jnp.concatenate([high, low, high, low], axis=1).astype(jnp.bfloat16)

    def four(s, first):
        return jnp.concatenate([v[s, first + j] for j in range(4)], axis=1)

    at_v = slice(32, 32 + levels)
    matrices1[0 : 4 * levels, :] = turned(jnp.where(even, e2[at_v, :], e1[at_v, :]))
    matrices1[4 * levels : 8 * levels, :] = turned(four(1, 0))
    matrices1[8 * levels : 12 * levels, :] = turned(four(1, 4))
    matrices1[12 * levels : 16 * levels, :] = turned(jnp.where(even, e1[at_v, :], e2[at_v, :]))
    matrices0[0 : 4 * levels, :] = turned(four(0, 0))
    matrices0[4 * levels : 8 * levels, :] = turned(four(0, 4))


def first_spread(levels, me_ref, *refs):
    messages, tables = refs[0:8], refs[8:16]
    part, m1, m2, acc, masks = refs[16:]
    per_field = 8 * levels
    me, lat_start, even = me_ref[0], me_ref[1], me_ref[2]
    acc[...] = jnp.zeros_like(acc)
    stay, back, on = lane_masks()
    for n, mask in enumerate((stay, back, jnp.zeros_like(stay), on)):
        masks[n] = mask
    for message, table in zip(messages, tables):

        def row(i, _, message=message, table=table):
            first = table[1, i].astype(jnp.int32) - lat_start + LOW
            tau = table[3, i].astype(jnp.int32)
            delta = (tau - me) & 3
            block = (tau + jnp.where(delta == 1, 7, jnp.where(delta == 3, 1, 0))) & 7
            weights = message[pl.ds(per_field + i, 8, stride=8), :]
            terms = masked(products(weights), masks[delta], range(NODES))
            sources = [rolled(message[pl.ds(8 * kk + i, 8, stride=8), :]) for kk in range(0, levels, 8)]
            add_terms(sources, terms, acc, (block // 4) * 15 + first)
            return 0

        lax.fori_loop(0, 8, row, 0, unroll=True)
    part[...] = acc[...].reshape(part.shape)

    def write(out, part_row, count):
        for h in range(2):
            out[h * 8 * levels : (h * 8 + count) * levels, :] = acc[
                h * 15 + part_row : h * 15 + part_row + count
            ].reshape(count * levels, 128)

    @pl.when(even == 1)
    def _():
        write(m1, 7, 8)
        write(m2, 0, 6)

    @pl.when(even == 0)
    def _():
        write(m2, 7, 8)
        write(m1, 0, 6)


def vertical(matrix, column):
    high = column.astype(jnp.bfloat16)
    low = (column - high.astype(jnp.float32)).astype(jnp.bfloat16)
    return jnp.dot(matrix, jnp.concatenate([high, high, low, low], axis=0), preferred_element_type=jnp.float32)


def second_spread(levels, me_ref, part, r1, r2, own_pack, y_pack, matrices, own_tab, y_tab, *refs):
    outs, (state, acc) = refs[0:8], refs[8:]
    me, lat_start, even, at_start, at_end = (me_ref[n] for n in range(5))
    slot = me // 4
    is_even = even == 1
    for n in range(15):
        halves = []
        for h in range(2):
            own = slice((h * 15 + n - 1) * levels, (h * 15 + n) * levels)
            b = slice((h * 8 + n) * levels, (h * 8 + n + 1) * levels)
            a = slice((h * 8 + n - 9) * levels, (h * 8 + n - 8) * levels)
            if n == 0:
                value = jnp.where(is_even, r2[b, :], r1[b, :])
            elif n < 8:
                value = part[own, :] + jnp.where(is_even, r2[b, :], r1[b, :])
            elif n == 8:
                value = part[own, :]
            else:
                value = part[own, :] + jnp.where(is_even, r1[a, :], r2[a, :])
            halves.append(value)
        result = vertical(matrices[n * levels : (n + 1) * levels, :], jnp.concatenate(halves, axis=1))
        state[n] = result[:, :128]
        state[15 + n] = result[:, 128:]
    for q in range(8):
        acc[q * 22 + 7 : q * 22 + 15] = jnp.zeros((8, levels, 128), jnp.float32)
    stay, back, on = lane_masks()

    def spread(n, h):
        mine = slot == h
        tau = jnp.where(mine, own_tab[2, n], y_tab[2, n]).astype(jnp.int32)
        first = jnp.where(mine, own_tab[0, n], y_tab[0, n]).astype(jnp.int32) - lat_start + 7
        at = slice(8 * n, 8 * n + 8)
        prods = products(jnp.where(mine, own_pack[at, :], y_pack[at, :]))
        sources = [rolled(state[h * 15 + n, kk : kk + 8, :]) for kk in range(0, levels, 8)]
        add_terms(sources, masked(prods, stay, range(NODES)), acc, (tau ^ me) * 22 + first)
        add_terms(sources, masked(prods, back, (0,)), acc, (((tau + 7) & 7) ^ me) * 22 + first)
        add_terms(sources, masked(prods, on, (2, 3)), acc, (((tau + 1) & 7) ^ me) * 22 + first)

    for n in range(4, 12):
        for h in range(2):
            spread(n, h)

    @pl.when(at_start == 0)
    def _():
        for n in range(4):
            for h in range(2):
                spread(n, h)

    @pl.when(at_end == 0)
    def _():
        for n in range(12, 15):
            for h in range(2):
                spread(n, h)

    for q in range(8):
        outs[q][...] = acc[q * 22 + 7 : q * 22 + 15].reshape(8 * levels, 128)


def finish(levels, me_ref, own, pair, across, up, diagonal, matrices, out):
    field = me_ref[0] // 4
    for i in range(8):
        rows = slice(i * levels, (i + 1) * levels)
        mine = own[rows, :] + pair[rows, :] + across[rows, :]
        other = up[rows, :] + diagonal[rows, :]
        result = vertical(matrices[rows, :], jnp.concatenate([mine, other], axis=1))
        for kk in range(0, levels, 8):
            out[pl.ds((field * levels + kk) * 8 + i, 8, stride=8), :] = result[kk : kk + 8, :128]
            out[pl.ds(((1 - field) * levels + kk) * 8 + i, 8, stride=8), :] = result[kk : kk + 8, 128:]


def swap_lon(value, bits):
    return lax.ppermute(value, "lon", [(i, i ^ bits) for i in range(RING)])


def swap_lat(value, odd):
    count = lax.axis_size("lat")
    pairs = [(i, i + 1) for i in range(odd, count - 1, 2)]
    return lax.ppermute(value, "lat", pairs + [(b, a) for a, b in pairs])


def ring_body(adjoint_in, lat_weights, lon_weights, depart_rows, depart_blocks, vertical_inverse):
    fields, levels, lat_rows, points = adjoint_in.shape
    me = lax.axis_index("lon")
    band = lax.axis_index("lat")
    count = lax.axis_size("lat")
    info = jnp.stack([me, band * lat_rows, 1 - band % 2, band == 0, band == count - 1]).astype(jnp.int32)
    per_field = 8 * levels
    size = adjoint_in.size
    message = per_field + 64 + 8
    side = 32 + levels + 8
    adjoint = adjoint_in.reshape(-1, points)
    lat_w, lon_w = lat_weights.reshape(-1, points), lon_weights.reshape(-1, points)
    sizes = [message, message, side, side]
    arguments = depart_rows[:, :, 0], depart_blocks[:, :, 0], adjoint, lat_w, lon_w, vertical_inverse
    own, other, e1, e2 = pl.pallas_call(
        functools.partial(assemble, levels),
        out_shape=[pltpu.VMEM((n, points), jnp.float32) for n in sizes],
        in_specs=[pl.BlockSpec(memory_space=pltpu.HBM)] * 6,
        out_specs=[pl.BlockSpec(memory_space=pltpu.VMEM)] * 4,
        scratch_shapes=[
            pltpu.VMEM((2, 2, 8), jnp.int32),
            pltpu.VMEM((32, points), jnp.float32),
            pltpu.VMEM((32, points), jnp.float32),
            pltpu.VMEM((8, levels, levels), jnp.float32),
            pltpu.SemaphoreType.DMA((16,)),
        ],
        compiler_params=pltpu.CompilerParams(vmem_limit_bytes=VMEM_LIMIT),
    )(*(pltpu.with_memory_space_constraint(value, pltpu.HBM) for value in arguments))
    far = {6: swap_lon(other, 6), 4: swap_lon(other, 4), 2: swap_lon(own, 2)}
    tile = pl.BlockSpec((8, 128), lambda i: (message // 8 - 1, 0), memory_space=pltpu.VMEM)
    e1, e2 = swap_lat(e1, 0), swap_lat(e2, 1)
    far[2], e1, e2 = lax.optimization_barrier((far[2], e1, e2))
    messages = [own, far[2], far[4], far[6]]
    messages = messages + [swap_lon(value, 1) for value in messages]
    part, m1, m2 = call(
        functools.partial(first_spread, levels),
        [30 * levels, 16 * levels, 16 * levels],
        [smem_whole(5)] + [vmem((message, 128))] * 8 + [smem_tile(message // 8 - 1)] * 8,
        [pltpu.VMEM((30, levels, 128), jnp.float32), pltpu.VMEM((4, 8, 128), jnp.float32)],
        8 * size,
        info,
        *messages,
        *messages,
    )
    r1, r2 = swap_lat(m1, 0), swap_lat(m2, 1)
    pack, matrices1, matrices0 = call(
        functools.partial(rim_data, levels),
        [128, (16 * levels, jnp.bfloat16), (8 * levels, jnp.bfloat16)],
        [smem_whole(5), tile, vmem((64, 128)), vmem((64, 128)), vmem((side, 128)), vmem((side, 128))]
        + [vmem(vertical_inverse.shape, 4), vmem((8, 128))],
        [],
        size,
        info,
        own,
        lat_w,
        lon_w,
        e1,
        e2,
        vertical_inverse,
        part,
    )
    y_pack = swap_lon(pack, 4)
    pieces = call(
        functools.partial(second_spread, levels),
        [8 * levels] * 8,
        [smem_whole(5), vmem((30 * levels, 128))]
        + [vmem((16 * levels, 128))] * 2
        + [vmem((128, 128))] * 2
        + [vmem((16 * levels, 128))]
        + [smem_tile(15)] * 2,
        [pltpu.VMEM((30, levels, 128), jnp.float32), pltpu.VMEM((8 * 22, levels, 128), jnp.float32)],
        16 * size,
        info,
        part,
        r1,
        r2,
        pack,
        y_pack,
        matrices1,
        pack,
        y_pack,
    )
    received = {}
    for bits in (6, 4, 2):
        received[bits] = swap_lon(pieces[bits] + swap_lon(pieces[bits + 1], 1), bits)
    pair = swap_lon(pieces[1], 1)
    (out,) = call(
        functools.partial(finish, levels),
        [fields * levels * 8],
        [smem_whole(5)] + [vmem((8 * levels, 128))] * 6,
        [],
        size,
        info,
        pieces[0],
        pair,
        received[2],
        received[4],
        received[6],
        matrices0,
    )
    return out.reshape(adjoint_in.shape)


def solution(mesh):
    specs = (
        P(None, None, "lat", "lon"),
        P(None, None, "lat", "lon"),
        P(None, None, "lat", "lon"),
        P(None, "lat", "lon"),
        P(None, "lat", "lon"),
        P(None, "lat", None, None),
    )

    def whole(*args):
        fields, levels, rows, points = args[0].shape
        lat, lon = mesh.shape["lat"], mesh.shape["lon"]
        ring = (fields, lon, rows // lat, points // lon) == (2, RING, 8, 128) and levels % 8 == 0 and levels * 4 == 128
        body = ring_body if ring else plain_body
        return jax.shard_map(body, mesh=mesh, in_specs=specs, out_specs=specs[0], check_vma=False)(*args)

    return whole
```

```python
import functools

import jax
import jax.numpy as jnp
from jax import lax
from jax.experimental import pallas as pl
from jax.experimental.pallas import tpu as pltpu
from jax.sharding import PartitionSpec as P

R = 2
H = 2
NODES = 4
RING = 8
LOW = H + 1
HIGH = H + 2
VMEM_LIMIT = 48 * 1024 * 1024


def shifted(array, axis, by):
    size = lax.axis_size(axis)
    return lax.ppermute(array, axis, [(i, (i + by) % size) for i in range(size)])


def from_behind(value, axis, steps):
    count = lax.axis_size(axis)
    leading, last = (max(0, -steps), min(count, count - steps))
    return lax.ppermute(value, axis, [(source, source + steps) for source in range(leading, last)])


def spread_local(carried, lat_w, lon_w, row_table, block_table, lat_start, own_block, cycle_size):
    fields, levels, lat_rows, points = carried.shape
    ext_rows = lat_rows + LOW + HIGH
    block_count = 2 * R + 3
    width = block_count * points
    rel_row = row_table - lat_start + LOW
    rel_block = (block_table - own_block + R) % cycle_size
    target = lax.broadcasted_iota(jnp.int32, (ext_rows, 4, lat_rows), 0)
    node = lax.broadcasted_iota(jnp.int32, (ext_rows, 4, lat_rows), 1)
    row_onehot = (target == rel_row[None, None, :] + node).astype(jnp.float32)
    placed_all = []
    for m in range(4):
        lon_row = jnp.zeros((fields, levels, lat_rows, points + 3), jnp.float32)
        for o in range(4):
            term = carried * (lat_w[m] * lon_w[o])[None, None]
            lon_row = lon_row + jnp.pad(term, ((0, 0), (0, 0), (0, 0), (o, 3 - o)))
        placed = jnp.zeros((fields, levels, lat_rows, width), jnp.float32)
        for d in range(2 * R + 1):
            left = (d + 1) * points - 1
            right = width - left - (points + 3)
            selected = (rel_block == d).astype(jnp.float32)[None, None, :, None]
            placed = placed + selected * jnp.pad(lon_row, ((0, 0), (0, 0), (0, 0), (left, right)))
        placed_all.append(placed)
    stacked = jnp.stack(placed_all, axis=2)
    return jnp.einsum("emj,fkmjc->fkec", row_onehot, stacked, precision=lax.Precision.HIGHEST)


def cycle_total(buffer, points):
    block_count = 2 * R + 3
    pieces = [buffer[..., q * points : (q + 1) * points] for q in range(block_count)]
    summed = pieces[R + 1]
    for q in range(block_count):
        if q != R + 1:
            summed = summed + shifted(pieces[q], "lon", q - R - 1)
    return summed


def fold_rims(buffer, lat_rows):
    upper = buffer[:, :, :LOW]
    lower = buffer[:, :, LOW + lat_rows :]
    interior = buffer[:, :, LOW : LOW + lat_rows]
    from_after = from_behind(upper, "lat", -1)
    from_before = from_behind(lower, "lat", 1)
    interior = interior + jnp.pad(from_after, ((0, 0), (0, 0), (lat_rows - LOW, 0), (0, 0)))
    interior = interior + jnp.pad(from_before, ((0, 0), (0, 0), (0, lat_rows - HIGH), (0, 0)))
    return interior


def plain_body(adjoint_in, lat_weights, lon_weights, depart_rows, depart_blocks, vertical_inverse):
    fields, levels, lat_rows, points = adjoint_in.shape
    cycle_size = lax.axis_size("lon")
    own_block = lax.axis_index("lon")
    lat_start = lax.axis_index("lat") * lat_rows
    carried = adjoint_in
    for s in (1, 0):
        partial_value = spread_local(
            carried,
            lat_weights[s],
            lon_weights[s],
            depart_rows[s, :, 0],
            depart_blocks[s, :, 0],
            lat_start,
            own_block,
            cycle_size,
        )
        gathered_rows = cycle_total(partial_value, points)
        interior = fold_rims(gathered_rows, lat_rows)
        carried = jnp.einsum(
            "imk,fmip->fkip", vertical_inverse[s], interior, precision=lax.Precision.HIGHEST
        )
    return carried


def vmem(shape, rank=2):
    return pl.BlockSpec(shape, lambda i: (0,) * rank, memory_space=pltpu.VMEM)


def smem_tile(tile):
    return pl.BlockSpec((8, 128), lambda i: (tile, 0), memory_space=pltpu.SMEM)


def smem_whole(size):
    return pl.BlockSpec((size,), lambda i: (0,), memory_space=pltpu.SMEM)


def call(kernel, outs, in_specs, scratch, cost, *args):
    outs = [((n, 128), jnp.float32) if isinstance(n, int) else n for n in outs]
    return pl.pallas_call(
        kernel,
        grid=(1,),
        out_shape=[jax.ShapeDtypeStruct(*out) for out in outs],
        in_specs=in_specs,
        out_specs=[vmem(shape, len(shape)) for shape, _ in outs],
        scratch_shapes=scratch,
        compiler_params=pltpu.CompilerParams(vmem_limit_bytes=VMEM_LIMIT),
        cost_estimate=pl.CostEstimate(flops=cost, bytes_accessed=cost, transcendentals=0),
    )(*args)


def rolled(value):
    return [pltpu.roll(value, 127, 1), value, pltpu.roll(value, 1, 1), pltpu.roll(value, 2, 1)]


def products(weights):
    turned = rolled(weights)
    return [turned[o][0:4] * turned[o][4 + o : 5 + o] for o in range(NODES)]


def lane_masks():
    lane = lax.broadcasted_iota(jnp.int32, (8, 128), 1)
    node = lax.broadcasted_iota(jnp.int32, (8, 128), 0)
    first = jnp.maximum(node - 1, 0)
    stay = (lane >= first) & (lane < jnp.where(node == 0, 127, 128))
    return [value.astype(jnp.float32) for value in (stay, (node == 0) & (lane == 127), (node >= 2) & (lane < first))]


def masked(prods, mask, nodes):
    return [(o, prods[o] * mask[o : o + 1]) for o in nodes]


def add_terms(sources, terms, target, first):
    for m in range(NODES):
        for kk, turned in enumerate(sources):
            total = None
            for o, weight in terms:
                term = turned[o] * weight[m : m + 1]
                total = term if total is None else total + term
            target[first + m, 8 * kk : 8 * kk + 8, :] += total


def assemble(levels, rows, blocks, adj, lat_w, lon_w, v, own, other, e1, e2, *scratch):
    tables, lat0, lon0, v1, sems = scratch
    field, even = lax.axis_index("lon") // 4, 1 - lax.axis_index("lat") % 2
    per_field = 8 * levels
    sem = iter(range(16))

    def copy(source, target):
        return pltpu.make_async_copy(source, target, sems.at[next(sem)])

    small = [copy(rows, tables.at[0]), copy(blocks, tables.at[1])]
    small += [copy(lat_w.at[pl.ds(0, 32)], lat0), copy(lon_w.at[pl.ds(0, 32)], lon0), copy(v.at[1], v1)]
    large = []
    for out, which in ((own, field), (other, 1 - field)):
        large.append(copy(adj.at[pl.ds(pl.multiple_of(which * per_field, per_field), per_field)], out.at[pl.ds(0, per_field)]))
        large.append(copy(lat_w.at[pl.ds(32, 32)], out.at[pl.ds(per_field, 32)]))
        large.append(copy(lon_w.at[pl.ds(32, 32)], out.at[pl.ds(per_field + 32, 32)]))
    for each in small + large:
        each.start()
    for each in small:
        each.wait()
    table = jnp.concatenate([tables[0], tables[1], tables[0], tables[1]], axis=0).astype(jnp.float32)
    for out, first in ((own, per_field + 64), (other, per_field + 64), (e1, 32 + levels), (e2, 32 + levels)):
        out[first : first + 8, 0:8] = table
    low = jnp.concatenate([v1[j] for j in range(4)], axis=1)
    high = jnp.concatenate([v1[j + 4] for j in range(4)], axis=1)
    for out, takes_high in ((e1, even == 1), (e2, even == 0)):
        first = jnp.where(takes_high, 4, 0)
        for i in range(4):
            out[8 * i : 8 * i + 4, :] = lat0[pl.ds(first + i, 4, stride=8), :]
            out[8 * i + 4 : 8 * i + 8, :] = lon0[pl.ds(first + i, 4, stride=8), :]
        out[32 : 32 + levels, :] = jnp.where(takes_high, high, low)
    for each in large:
        each.wait()


def rim_data(levels, me_ref, own_tile, lat_w, lon_w, e1, e2, v, after_this, pack, matrices1, matrices0):
    even = me_ref[2] == 1
    for i in range(8):
        pack[32 + 8 * i : 36 + 8 * i, :] = lat_w[pl.ds(i, 4, stride=8), :]
        pack[36 + 8 * i : 40 + 8 * i, :] = lon_w[pl.ds(i, 4, stride=8), :]
    pack[0:32, :] = jnp.where(even, e2[0:32, :], e1[0:32, :])
    pack[96:120, :] = jnp.where(even, e1[0:24, :], e2[0:24, :])
    tab = slice(32 + levels, 40 + levels)
    before = pltpu.roll(jnp.where(even, e2[tab, :], e1[tab, :]), 124, 1)
    after = pltpu.roll(jnp.where(even, e1[tab, :], e2[tab, :]), 12, 1)
    lane = lax.broadcasted_iota(jnp.int32, (8, 128), 1)
    pack[120:128, :] = jnp.where(lane < 4, before, jnp.where(lane < 12, pltpu.roll(own_tile[...], 4, 1), after))

    def turned(four):
        value = four.T
        high = value.astype(jnp.bfloat16).astype(jnp.float32)
        low = value - high
        return jnp.concatenate([high, low, high, low], axis=1).astype(jnp.bfloat16)

    def four(s, first):
        return jnp.concatenate([v[s, first + j] for j in range(4)], axis=1)

    at_v = slice(32, 32 + levels)
    matrices1[0 : 4 * levels, :] = turned(jnp.where(even, e2[at_v, :], e1[at_v, :]))
    matrices1[4 * levels : 8 * levels, :] = turned(four(1, 0))
    matrices1[8 * levels : 12 * levels, :] = turned(four(1, 4))
    matrices1[12 * levels : 16 * levels, :] = turned(jnp.where(even, e1[at_v, :], e2[at_v, :]))
    matrices0[0 : 4 * levels, :] = turned(four(0, 0))
    matrices0[4 * levels : 8 * levels, :] = turned(four(0, 4))


def spread_messages(levels, me_ref, messages, tables, acc, masks):
    per_field = 8 * levels
    me, lat_start = me_ref[0], me_ref[1]
    stay, back, on = lane_masks()
    for n, mask in enumerate((stay, back, jnp.zeros_like(stay), on)):
        masks[n] = mask
    for message, table in zip(messages, tables):

        def row(i, _, message=message, table=table):
            first = table[1, i].astype(jnp.int32) - lat_start + LOW
            tau = table[3, i].astype(jnp.int32)
            delta = (tau - me) & 3
            block = (tau + jnp.where(delta == 1, 7, jnp.where(delta == 3, 1, 0))) & 7
            weights = message[pl.ds(per_field + i, 8, stride=8), :]
            terms = masked(products(weights), masks[delta], range(NODES))
            sources = [rolled(message[pl.ds(8 * kk + i, 8, stride=8), :]) for kk in range(0, levels, 8)]
            add_terms(sources, terms, acc, (block // 4) * 15 + first)
            return 0

        lax.fori_loop(0, 8, row, 0, unroll=True)


def first_spread_own(levels, me_ref, *refs):
    messages, tables, (acc, masks) = refs[0:4], refs[4:8], refs[8:]
    acc[...] = jnp.zeros_like(acc)
    spread_messages(levels, me_ref, messages, tables, acc, masks)


def first_spread_other(levels, me_ref, *refs):
    messages, tables, (before, acc, m1, m2, masks) = refs[0:4], refs[4:8], refs[8:]
    acc[...] = before[...]
    spread_messages(levels, me_ref, messages, tables, acc, masks)
    even = me_ref[2]

    def write(out, part_row, count):
        for h in range(2):
            out[h * 8 * levels : (h * 8 + count) * levels, :] = acc[
                h * 15 + part_row : h * 15 + part_row + count
            ].reshape(count * levels, 128)

    @pl.when(even == 1)
    def _():
        write(m1, 7, 8)
        write(m2, 0, 6)

    @pl.when(even == 0)
    def _():
        write(m2, 7, 8)
        write(m1, 0, 6)


def vertical(matrix, column):
    high = column.astype(jnp.bfloat16)
    low = (column - high.astype(jnp.float32)).astype(jnp.bfloat16)
    return jnp.dot(matrix, jnp.concatenate([high, high, low, low], axis=0), preferred_element_type=jnp.float32)


def spread_half(levels, upper, me_ref, part, received, own_pack, y_pack, matrices, own_tab, y_tab, state, acc):
    me, lat_start, at_start, at_end = me_ref[0], me_ref[1], me_ref[3], me_ref[4]
    slot = me // 4
    base = 8 * upper

    def exists(j):
        n = base + j
        there = (n < 15) & ((at_start == 0) | (n >= 4)) if j < 4 else n < 15
        return there & ((at_end == 0) | (n < 12)) if j >= 4 else there

    for j in range(8):
        halves = []
        for h in range(2):
            sent = received[pl.ds(pl.multiple_of((h * 8 + j - upper) * levels, levels) if j else h * 8 * levels, levels), :]
            if j == 0:
                value = jnp.where(upper == 1, part[h * 15 + 7], sent)
            else:
                value = part[h * 15 + base + j - 1] + sent
            if j == 7:
                value = jnp.where(upper == 1, 0.0, value)
            halves.append(value)
        matrix = matrices[pl.ds(pl.multiple_of((base + j) * levels, levels), levels), :]
        result = vertical(matrix, jnp.concatenate(halves, axis=1))
        state[j] = result[:, :128]
        state[8 + j] = result[:, 128:]
    for q in range(8):
        acc[q * 22 + 7 : q * 22 + 15] = jnp.zeros((8, levels, 128), jnp.float32)
    stay, back, on = lane_masks()
    for j in range(8):
        n = base + j
        there = exists(j)
        at = pl.ds(pl.multiple_of(8 * n, 8), 8)
        for h in range(2):
            mine = slot == h
            tau = jnp.where(there, jnp.where(mine, own_tab[2, n], y_tab[2, n]).astype(jnp.int32), 0)
            first = jnp.where(mine, own_tab[0, n], y_tab[0, n]).astype(jnp.int32) - lat_start + 7
            first = jnp.where(there, first, 7)
            prods = products(jnp.where(there, jnp.where(mine, own_pack[at, :], y_pack[at, :]), 0.0))
            sources = [rolled(state[h * 8 + j, kk : kk + 8, :]) for kk in range(0, levels, 8)]
            add_terms(sources, masked(prods, stay, range(NODES)), acc, (tau ^ me) * 22 + first)
            add_terms(sources, masked(prods, back, (0,)), acc, (((tau + 7) & 7) ^ me) * 22 + first)
            add_terms(sources, masked(prods, on, (2, 3)), acc, (((tau + 1) & 7) ^ me) * 22 + first)


def second_spread_early(levels, me_ref, *refs):
    (acc, state), refs = refs[-2:], refs[:-2]
    spread_half(levels, me_ref[2], me_ref, *refs, state, acc)


def second_spread_late(levels, me_ref, *refs):
    (before, *outs, state, acc), refs = refs[7:], refs[:7]
    spread_half(levels, 1 - me_ref[2], me_ref, *refs, state, acc)
    for q, out in enumerate(outs):
        rows = slice(q * 22 + 7, q * 22 + 15)
        out[...] = (acc[rows] + before[rows]).reshape(8 * levels, 128)


def finish(levels, me_ref, own, pair, across, up, diagonal, matrices, out):
    field = me_ref[0] // 4
    for i in range(8):
        rows = slice(i * levels, (i + 1) * levels)
        mine = own[rows, :] + pair[rows, :] + across[rows, :]
        other = up[rows, :] + diagonal[rows, :]
        result = vertical(matrices[rows, :], jnp.concatenate([mine, other], axis=1))
        for kk in range(0, levels, 8):
            out[pl.ds((field * levels + kk) * 8 + i, 8, stride=8), :] = result[kk : kk + 8, :128]
            out[pl.ds(((1 - field) * levels + kk) * 8 + i, 8, stride=8), :] = result[kk : kk + 8, 128:]


def swap_lon(value, bits):
    return lax.ppermute(value, "lon", [(i, i ^ bits) for i in range(RING)])


def swap_lat(value, odd):
    count = lax.axis_size("lat")
    pairs = [(i, i + 1) for i in range(odd, count - 1, 2)]
    return lax.ppermute(value, "lat", pairs + [(b, a) for a, b in pairs])


def ring_body(adjoint_in, lat_weights, lon_weights, depart_rows, depart_blocks, vertical_inverse):
    fields, levels, lat_rows, points = adjoint_in.shape
    me = lax.axis_index("lon")
    band = lax.axis_index("lat")
    count = lax.axis_size("lat")
    info = jnp.stack([me, band * lat_rows, 1 - band % 2, band == 0, band == count - 1]).astype(jnp.int32)
    per_field = 8 * levels
    size = adjoint_in.size
    message = per_field + 64 + 8
    side = 32 + levels + 8
    adjoint = adjoint_in.reshape(-1, points)
    lat_w, lon_w = lat_weights.reshape(-1, points), lon_weights.reshape(-1, points)
    sizes = [message, message, side, side]
    arguments = depart_rows[:, :, 0], depart_blocks[:, :, 0], adjoint, lat_w, lon_w, vertical_inverse
    own, other, e1, e2 = pl.pallas_call(
        functools.partial(assemble, levels),
        out_shape=[pltpu.VMEM((n, points), jnp.float32) for n in sizes],
        in_specs=[pl.BlockSpec(memory_space=pltpu.HBM)] * 6,
        out_specs=[pl.BlockSpec(memory_space=pltpu.VMEM)] * 4,
        scratch_shapes=[
            pltpu.VMEM((2, 2, 8), jnp.int32),
            pltpu.VMEM((32, points), jnp.float32),
            pltpu.VMEM((32, points), jnp.float32),
            pltpu.VMEM((8, levels, levels), jnp.float32),
            pltpu.SemaphoreType.DMA((16,)),
        ],
        compiler_params=pltpu.CompilerParams(vmem_limit_bytes=VMEM_LIMIT),
    )(*(pltpu.with_memory_space_constraint(value, pltpu.HBM) for value in arguments))
    far = {6: swap_lon(other, 6), 4: swap_lon(other, 4), 2: swap_lon(own, 2)}
    tile = pl.BlockSpec((8, 128), lambda i: (message // 8 - 1, 0), memory_space=pltpu.VMEM)
    e1, e2 = swap_lat(e1, 0), swap_lat(e2, 1)
    far[2], e1, e2 = lax.optimization_barrier((far[2], e1, e2))
    messages = [own, far[2], far[4], far[6]]
    messages = messages + [swap_lon(value, 1) for value in messages]
    table = smem_tile(message // 8 - 1)
    masks = pltpu.VMEM((4, 8, 128), jnp.float32)
    partial = ((30, levels, 128), jnp.float32)
    (part,) = call(
        functools.partial(first_spread_own, levels),
        [partial],
        [smem_whole(5)] + [vmem((message, 128))] * 4 + [table] * 4,
        [masks],
        8 * size,
        info,
        *messages[:4],
        *messages[:4],
    )
    part, m1, m2 = call(
        functools.partial(first_spread_other, levels),
        [partial, 16 * levels, 16 * levels],
        [smem_whole(5)] + [vmem((message, 128))] * 4 + [table] * 4 + [vmem(partial[0], 3)],
        [masks],
        8 * size,
        info,
        *messages[4:],
        *messages[4:],
        part,
    )
    r1, r2 = swap_lat(m1, 0), swap_lat(m2, 1)
    pack, matrices1, matrices0 = call(
        functools.partial(rim_data, levels),
        [128, ((16 * levels, 128), jnp.bfloat16), ((8 * levels, 128), jnp.bfloat16)],
        [smem_whole(5), tile, vmem((64, 128)), vmem((64, 128)), vmem((side, 128)), vmem((side, 128))]
        + [vmem(vertical_inverse.shape, 4), vmem((8, levels, 128), 3)],
        [],
        size,
        info,
        own,
        lat_w,
        lon_w,
        e1,
        e2,
        vertical_inverse,
        part,
    )
    y_pack = swap_lon(pack, 4)
    half_specs = [smem_whole(5), vmem(partial[0], 3), vmem((16 * levels, 128)), vmem((128, 128)), vmem((128, 128))]
    half_specs += [vmem((16 * levels, 128)), smem_tile(15), smem_tile(15)]
    spread_shape = ((8 * 22, levels, 128), jnp.float32)
    state = pltpu.VMEM((16, levels, 128), jnp.float32)
    (early,) = call(
        functools.partial(second_spread_early, levels),
        [spread_shape],
        half_specs,
        [state],
        8 * size,
        *(info, part, r1, pack, y_pack, matrices1, pack, y_pack),
    )
    pieces = call(
        functools.partial(second_spread_late, levels),
        [8 * levels] * 8,
        half_specs + [vmem(spread_shape[0], 3)],
        [state, pltpu.VMEM(*spread_shape)],
        8 * size,
        *(info, part, r2, pack, y_pack, matrices1, pack, y_pack, early),
    )
    received = {}
    for bits in (6, 4, 2):
        received[bits] = swap_lon(pieces[bits] + swap_lon(pieces[bits + 1], 1), bits)
    pair = swap_lon(pieces[1], 1)
    (out,) = call(
        functools.partial(finish, levels),
        [fields * levels * 8],
        [smem_whole(5)] + [vmem((8 * levels, 128))] * 6,
        [],
        size,
        info,
        pieces[0],
        pair,
        received[2],
        received[4],
        received[6],
        matrices0,
    )
    return out.reshape(adjoint_in.shape)


def solution(mesh):
    specs = (
        P(None, None, "lat", "lon"),
        P(None, None, "lat", "lon"),
        P(None, None, "lat", "lon"),
        P(None, "lat", "lon"),
        P(None, "lat", "lon"),
        P(None, "lat", None, None),
    )

    def whole(*args):
        fields, levels, rows, points = args[0].shape
        lat, lon = mesh.shape["lat"], mesh.shape["lon"]
        ring = (fields, lon, rows // lat, points // lon) == (2, RING, 8, 128) and levels % 8 == 0 and levels * 4 == 128
        body = ring_body if ring else plain_body
        return jax.shard_map(body, mesh=mesh, in_specs=specs, out_specs=specs[0], check_vma=False)(*args)

    return whole
```

```python
import functools

import jax
import jax.numpy as jnp
from jax import lax
from jax.experimental import pallas as pl
from jax.experimental.pallas import tpu as pltpu
from jax.sharding import PartitionSpec as P

R = 2
H = 2
NODES = 4
RING = 8
LOW = H + 1
HIGH = H + 2
VMEM_LIMIT = 48 * 1024 * 1024


def shifted(array, axis, by):
    size = lax.axis_size(axis)
    return lax.ppermute(array, axis, [(i, (i + by) % size) for i in range(size)])


def from_behind(value, axis, steps):
    count = lax.axis_size(axis)
    leading, last = (max(0, -steps), min(count, count - steps))
    return lax.ppermute(value, axis, [(source, source + steps) for source in range(leading, last)])


def spread_local(carried, lat_w, lon_w, row_table, block_table, lat_start, own_block, cycle_size):
    fields, levels, lat_rows, points = carried.shape
    ext_rows = lat_rows + LOW + HIGH
    block_count = 2 * R + 3
    width = block_count * points
    rel_row = row_table - lat_start + LOW
    rel_block = (block_table - own_block + R) % cycle_size
    target = lax.broadcasted_iota(jnp.int32, (ext_rows, 4, lat_rows), 0)
    node = lax.broadcasted_iota(jnp.int32, (ext_rows, 4, lat_rows), 1)
    row_onehot = (target == rel_row[None, None, :] + node).astype(jnp.float32)
    placed_all = []
    for m in range(4):
        lon_row = jnp.zeros((fields, levels, lat_rows, points + 3), jnp.float32)
        for o in range(4):
            term = carried * (lat_w[m] * lon_w[o])[None, None]
            lon_row = lon_row + jnp.pad(term, ((0, 0), (0, 0), (0, 0), (o, 3 - o)))
        placed = jnp.zeros((fields, levels, lat_rows, width), jnp.float32)
        for d in range(2 * R + 1):
            left = (d + 1) * points - 1
            right = width - left - (points + 3)
            selected = (rel_block == d).astype(jnp.float32)[None, None, :, None]
            placed = placed + selected * jnp.pad(lon_row, ((0, 0), (0, 0), (0, 0), (left, right)))
        placed_all.append(placed)
    stacked = jnp.stack(placed_all, axis=2)
    return jnp.einsum("emj,fkmjc->fkec", row_onehot, stacked, precision=lax.Precision.HIGHEST)


def cycle_total(buffer, points):
    block_count = 2 * R + 3
    pieces = [buffer[..., q * points : (q + 1) * points] for q in range(block_count)]
    summed = pieces[R + 1]
    for q in range(block_count):
        if q != R + 1:
            summed = summed + shifted(pieces[q], "lon", q - R - 1)
    return summed


def fold_rims(buffer, lat_rows):
    upper = buffer[:, :, :LOW]
    lower = buffer[:, :, LOW + lat_rows :]
    interior = buffer[:, :, LOW : LOW + lat_rows]
    from_after = from_behind(upper, "lat", -1)
    from_before = from_behind(lower, "lat", 1)
    interior = interior + jnp.pad(from_after, ((0, 0), (0, 0), (lat_rows - LOW, 0), (0, 0)))
    interior = interior + jnp.pad(from_before, ((0, 0), (0, 0), (0, lat_rows - HIGH), (0, 0)))
    return interior


def plain_body(adjoint_in, lat_weights, lon_weights, depart_rows, depart_blocks, vertical_inverse):
    fields, levels, lat_rows, points = adjoint_in.shape
    cycle_size = lax.axis_size("lon")
    own_block = lax.axis_index("lon")
    lat_start = lax.axis_index("lat") * lat_rows
    carried = adjoint_in
    for s in (1, 0):
        partial_value = spread_local(
            carried,
            lat_weights[s],
            lon_weights[s],
            depart_rows[s, :, 0],
            depart_blocks[s, :, 0],
            lat_start,
            own_block,
            cycle_size,
        )
        gathered_rows = cycle_total(partial_value, points)
        interior = fold_rims(gathered_rows, lat_rows)
        carried = jnp.einsum(
            "imk,fmip->fkip", vertical_inverse[s], interior, precision=lax.Precision.HIGHEST
        )
    return carried


def vmem(shape, rank=2):
    return pl.BlockSpec(shape, lambda i: (0,) * rank, memory_space=pltpu.VMEM)


def smem_tile(tile):
    return pl.BlockSpec((8, 128), lambda i: (tile, 0), memory_space=pltpu.SMEM)


def call(kernel, outs, in_specs, scratch, cost, *args):
    outs = [((n, 128), jnp.float32) if isinstance(n, int) else n for n in outs]
    return pl.pallas_call(
        kernel,
        grid=(1,),
        out_shape=[jax.ShapeDtypeStruct(*out) for out in outs],
        in_specs=in_specs,
        out_specs=[vmem(shape, len(shape)) for shape, _ in outs],
        scratch_shapes=scratch,
        compiler_params=pltpu.CompilerParams(vmem_limit_bytes=VMEM_LIMIT),
        cost_estimate=pl.CostEstimate(flops=cost, bytes_accessed=cost, transcendentals=0),
    )(*args)


def even_band():
    return 1 - lax.axis_index("lat") % 2


def rolled(value):
    return [pltpu.roll(value, 127, 1), value, pltpu.roll(value, 1, 1), pltpu.roll(value, 2, 1)]


def products(weights):
    turned = rolled(weights)
    return [turned[o][0:4] * turned[o][4 + o : 5 + o] for o in range(NODES)]


def lane_masks():
    lane = lax.broadcasted_iota(jnp.int32, (8, 128), 1)
    node = lax.broadcasted_iota(jnp.int32, (8, 128), 0)
    first = jnp.maximum(node - 1, 0)
    stay = (lane >= first) & (lane < jnp.where(node == 0, 127, 128))
    return [value.astype(jnp.float32) for value in (stay, (node == 0) & (lane == 127), (node >= 2) & (lane < first))]


def masked(prods, mask, nodes):
    return [(o, prods[o] * mask[o : o + 1]) for o in nodes]


def add_terms(sources, terms, target, first):
    for m in range(NODES):
        for kk, turned in enumerate(sources):
            total = None
            for o, weight in terms:
                term = turned[o] * weight[m : m + 1]
                total = term if total is None else total + term
            target[first + m, 8 * kk : 8 * kk + 8, :] += total


def assemble(levels, rows, blocks, adj, lat_w, lon_w, v, own, other, e1, e2, *scratch):
    tables, lat0, lon0, v1, sems = scratch
    field, even = lax.axis_index("lon") // 4, even_band()
    per_field = 8 * levels
    sem = iter(range(16))

    def copy(source, target):
        return pltpu.make_async_copy(source, target, sems.at[next(sem)])

    small = [copy(rows, tables.at[0]), copy(blocks, tables.at[1])]
    small += [copy(lat_w.at[pl.ds(0, 32)], lat0), copy(lon_w.at[pl.ds(0, 32)], lon0), copy(v.at[1], v1)]
    large = []
    for out, which in ((own, field), (other, 1 - field)):
        large.append(copy(adj.at[pl.ds(pl.multiple_of(which * per_field, per_field), per_field)], out.at[pl.ds(0, per_field)]))
        large.append(copy(lat_w.at[pl.ds(32, 32)], out.at[pl.ds(per_field, 32)]))
        large.append(copy(lon_w.at[pl.ds(32, 32)], out.at[pl.ds(per_field + 32, 32)]))
    for each in small + large:
        each.start()
    for each in small:
        each.wait()
    table = jnp.concatenate([tables[0], tables[1], tables[0], tables[1]], axis=0).astype(jnp.float32)
    for out, first in ((own, per_field + 64), (other, per_field + 64), (e1, 32 + levels), (e2, 32 + levels)):
        out[first : first + 8, 0:8] = table
    low = jnp.concatenate([v1[j] for j in range(4)], axis=1)
    high = jnp.concatenate([v1[j + 4] for j in range(4)], axis=1)
    for out, takes_high in ((e1, even == 1), (e2, even == 0)):
        first = jnp.where(takes_high, 4, 0)
        for i in range(4):
            out[8 * i : 8 * i + 4, :] = lat0[pl.ds(first + i, 4, stride=8), :]
            out[8 * i + 4 : 8 * i + 8, :] = lon0[pl.ds(first + i, 4, stride=8), :]
        out[32 : 32 + levels, :] = jnp.where(takes_high, high, low)
    for each in large:
        each.wait()


def rim_data(levels, own_tile, lat_w, lon_w, e1, e2, v, after_this, pack, matrices1, matrices0):
    even = even_band() == 1
    for i in range(8):
        pack[32 + 8 * i : 36 + 8 * i, :] = lat_w[pl.ds(i, 4, stride=8), :]
        pack[36 + 8 * i : 40 + 8 * i, :] = lon_w[pl.ds(i, 4, stride=8), :]
    pack[0:32, :] = jnp.where(even, e2[0:32, :], e1[0:32, :])
    pack[96:120, :] = jnp.where(even, e1[0:24, :], e2[0:24, :])
    tab = slice(32 + levels, 40 + levels)
    before = pltpu.roll(jnp.where(even, e2[tab, :], e1[tab, :]), 124, 1)
    after = pltpu.roll(jnp.where(even, e1[tab, :], e2[tab, :]), 12, 1)
    lane = lax.broadcasted_iota(jnp.int32, (8, 128), 1)
    pack[120:128, :] = jnp.where(lane < 4, before, jnp.where(lane < 12, pltpu.roll(own_tile[...], 4, 1), after))

    def turned(four):
        value = four.T
        high = value.astype(jnp.bfloat16).astype(jnp.float32)
        low = value - high
        return jnp.concatenate([high, low, high, low], axis=1).astype(jnp.bfloat16)

    def four(s, first):
        return jnp.concatenate([v[s, first + j] for j in range(4)], axis=1)

    at_v = slice(32, 32 + levels)
    matrices1[0 : 4 * levels, :] = turned(jnp.where(even, e2[at_v, :], e1[at_v, :]))
    matrices1[4 * levels : 8 * levels, :] = turned(four(1, 0))
    matrices1[8 * levels : 12 * levels, :] = turned(four(1, 4))
    matrices1[12 * levels : 16 * levels, :] = turned(jnp.where(even, e1[at_v, :], e2[at_v, :]))
    matrices0[0 : 4 * levels, :] = turned(four(0, 0))
    matrices0[4 * levels : 8 * levels, :] = turned(four(0, 4))


def spread_messages(levels, messages, tables, acc, masks):
    per_field = 8 * levels
    me, lat_start = lax.axis_index("lon"), 8 * lax.axis_index("lat")
    stay, back, on = lane_masks()
    for n, mask in enumerate((stay, back, jnp.zeros_like(stay), on)):
        masks[n] = mask
    for message, table in zip(messages, tables):

        def row(i, _, message=message, table=table):
            first = table[1, i].astype(jnp.int32) - lat_start + LOW
            tau = table[3, i].astype(jnp.int32)
            delta = (tau - me) & 3
            block = (tau + jnp.where(delta == 1, 7, jnp.where(delta == 3, 1, 0))) & 7
            weights = message[pl.ds(per_field + i, 8, stride=8), :]
            terms = masked(products(weights), masks[delta], range(NODES))
            sources = [rolled(message[pl.ds(8 * kk + i, 8, stride=8), :]) for kk in range(0, levels, 8)]
            add_terms(sources, terms, acc, (block // 4) * 15 + first)
            return 0

        lax.fori_loop(0, 8, row, 0, unroll=True)


def first_spread_own(levels, *refs):
    messages, tables, (acc, masks) = refs[0:4], refs[4:8], refs[8:]
    acc[...] = jnp.zeros_like(acc)
    spread_messages(levels, messages, tables, acc, masks)


def first_spread_other(levels, *refs):
    messages, tables, (before, acc, m1, m2, masks) = refs[0:4], refs[4:8], refs[8:]
    acc[...] = before[...]
    spread_messages(levels, messages, tables, acc, masks)
    even = even_band()

    def write(out, part_row, count):
        for h in range(2):
            out[h * 8 * levels : (h * 8 + count) * levels, :] = acc[
                h * 15 + part_row : h * 15 + part_row + count
            ].reshape(count * levels, 128)

    @pl.when(even == 1)
    def _():
        write(m1, 7, 8)
        write(m2, 0, 6)

    @pl.when(even == 0)
    def _():
        write(m2, 7, 8)
        write(m1, 0, 6)


def vertical(matrix, column):
    high = column.astype(jnp.bfloat16)
    low = (column - high.astype(jnp.float32)).astype(jnp.bfloat16)
    return jnp.dot(matrix, jnp.concatenate([high, high, low, low], axis=0), preferred_element_type=jnp.float32)


def spread_half(levels, upper, part, received, own_pack, y_pack, matrices, own_tab, y_tab, state, acc):
    me, band = lax.axis_index("lon"), lax.axis_index("lat")
    lat_start, at_start, at_end = 8 * band, band == 0, band == lax.axis_size("lat") - 1
    slot = me // 4
    base = 8 * upper

    def exists(j):
        n = base + j
        there = (n < 15) & (~at_start | (n >= 4)) if j < 4 else n < 15
        return there & (~at_end | (n < 12)) if j >= 4 else there

    for j in range(8):
        halves = []
        for h in range(2):
            sent = received[pl.ds(pl.multiple_of((h * 8 + j - upper) * levels, levels) if j else h * 8 * levels, levels), :]
            if j == 0:
                value = jnp.where(upper == 1, part[h * 15 + 7], sent)
            else:
                value = part[h * 15 + base + j - 1] + sent
            if j == 7:
                value = jnp.where(upper == 1, 0.0, value)
            halves.append(value)
        matrix = matrices[pl.ds(pl.multiple_of((base + j) * levels, levels), levels), :]
        result = vertical(matrix, jnp.concatenate(halves, axis=1))
        state[j] = result[:, :128]
        state[8 + j] = result[:, 128:]
    for q in range(8):
        acc[q * 22 + 7 : q * 22 + 15] = jnp.zeros((8, levels, 128), jnp.float32)
    stay, back, on = lane_masks()
    for j in range(8):
        n = base + j
        there = exists(j)
        at = pl.ds(pl.multiple_of(8 * n, 8), 8)
        for h in range(2):
            mine = slot == h
            tau = jnp.where(there, jnp.where(mine, own_tab[2, n], y_tab[2, n]).astype(jnp.int32), 0)
            first = jnp.where(mine, own_tab[0, n], y_tab[0, n]).astype(jnp.int32) - lat_start + 7
            first = jnp.where(there, first, 7)
            prods = products(jnp.where(there, jnp.where(mine, own_pack[at, :], y_pack[at, :]), 0.0))
            sources = [rolled(state[h * 8 + j, kk : kk + 8, :]) for kk in range(0, levels, 8)]
            add_terms(sources, masked(prods, stay, range(NODES)), acc, (tau ^ me) * 22 + first)
            add_terms(sources, masked(prods, back, (0,)), acc, (((tau + 7) & 7) ^ me) * 22 + first)
            add_terms(sources, masked(prods, on, (2, 3)), acc, (((tau + 1) & 7) ^ me) * 22 + first)


def second_spread_early(levels, *refs):
    (acc, state), refs = refs[-2:], refs[:-2]
    spread_half(levels, even_band(), *refs, state, acc)


def second_spread_late(levels, *refs):
    (before, *outs, state, acc), refs = refs[7:], refs[:7]
    spread_half(levels, 1 - even_band(), *refs, state, acc)
    for q, out in enumerate(outs):
        rows = slice(q * 22 + 7, q * 22 + 15)
        out[...] = (acc[rows] + before[rows]).reshape(8 * levels, 128)


def finish(levels, own, pair, across, up, diagonal, matrices, out):
    field = lax.axis_index("lon") // 4
    for i in range(8):
        rows = slice(i * levels, (i + 1) * levels)
        mine = own[rows, :] + pair[rows, :] + across[rows, :]
        other = up[rows, :] + diagonal[rows, :]
        result = vertical(matrices[rows, :], jnp.concatenate([mine, other], axis=1))
        for kk in range(0, levels, 8):
            out[pl.ds((field * levels + kk) * 8 + i, 8, stride=8), :] = result[kk : kk + 8, :128]
            out[pl.ds(((1 - field) * levels + kk) * 8 + i, 8, stride=8), :] = result[kk : kk + 8, 128:]


def swap_lon(value, bits):
    return lax.ppermute(value, "lon", [(i, i ^ bits) for i in range(RING)])


def swap_lat(value, odd):
    count = lax.axis_size("lat")
    pairs = [(i, i + 1) for i in range(odd, count - 1, 2)]
    return lax.ppermute(value, "lat", pairs + [(b, a) for a, b in pairs])


def ring_body(adjoint_in, lat_weights, lon_weights, depart_rows, depart_blocks, vertical_inverse):
    fields, levels, lat_rows, points = adjoint_in.shape
    per_field = 8 * levels
    size = adjoint_in.size
    message = per_field + 64 + 8
    side = 32 + levels + 8
    adjoint = adjoint_in.reshape(-1, points)
    lat_w, lon_w = lat_weights.reshape(-1, points), lon_weights.reshape(-1, points)
    sizes = [message, message, side, side]
    arguments = depart_rows[:, :, 0], depart_blocks[:, :, 0], adjoint, lat_w, lon_w, vertical_inverse
    own, other, e1, e2 = pl.pallas_call(
        functools.partial(assemble, levels),
        out_shape=[pltpu.VMEM((n, points), jnp.float32) for n in sizes],
        in_specs=[pl.BlockSpec(memory_space=pltpu.HBM)] * 6,
        out_specs=[pl.BlockSpec(memory_space=pltpu.VMEM)] * 4,
        scratch_shapes=[
            pltpu.VMEM((2, 2, 8), jnp.int32),
            pltpu.VMEM((32, points), jnp.float32),
            pltpu.VMEM((32, points), jnp.float32),
            pltpu.VMEM((8, levels, levels), jnp.float32),
            pltpu.SemaphoreType.DMA((16,)),
        ],
        compiler_params=pltpu.CompilerParams(vmem_limit_bytes=VMEM_LIMIT),
    )(*(pltpu.with_memory_space_constraint(value, pltpu.HBM) for value in arguments))
    far = {2: swap_lon(own, 2), 4: swap_lon(other, 4), 6: swap_lon(other, 6)}
    tile = pl.BlockSpec((8, 128), lambda i: (message // 8 - 1, 0), memory_space=pltpu.VMEM)
    e1, e2 = swap_lat(e1, 0), swap_lat(e2, 1)
    far[4], e1, e2 = lax.optimization_barrier((far[4], e1, e2))
    messages = [own, far[2], far[4], far[6]]
    messages = messages + [swap_lon(value, 1) for value in messages]
    table = smem_tile(message // 8 - 1)
    masks = pltpu.VMEM((4, 8, 128), jnp.float32)
    partial = ((30, levels, 128), jnp.float32)
    (part,) = call(
        functools.partial(first_spread_own, levels),
        [partial],
        [vmem((message, 128))] * 4 + [table] * 4,
        [masks],
        8 * size,
        *messages[:4],
        *messages[:4],
    )
    part, m1, m2 = call(
        functools.partial(first_spread_other, levels),
        [partial, 16 * levels, 16 * levels],
        [vmem((message, 128))] * 4 + [table] * 4 + [vmem(partial[0], 3)],
        [masks],
        8 * size,
        *messages[4:],
        *messages[4:],
        part,
    )
    r1, r2 = swap_lat(m1, 0), swap_lat(m2, 1)
    pack, matrices1, matrices0 = call(
        functools.partial(rim_data, levels),
        [128, ((16 * levels, 128), jnp.bfloat16), ((8 * levels, 128), jnp.bfloat16)],
        [tile, vmem((64, 128)), vmem((64, 128)), vmem((side, 128)), vmem((side, 128))]
        + [vmem(vertical_inverse.shape, 4), vmem((8, levels, 128), 3)],
        [],
        size,
        own,
        lat_w,
        lon_w,
        e1,
        e2,
        vertical_inverse,
        part,
    )
    y_pack = swap_lon(pack, 4)
    half_specs = [vmem(partial[0], 3), vmem((16 * levels, 128)), vmem((128, 128)), vmem((128, 128))]
    half_specs += [vmem((16 * levels, 128)), smem_tile(15), smem_tile(15)]
    spread_shape = ((8 * 22, levels, 128), jnp.float32)
    state = pltpu.VMEM((16, levels, 128), jnp.float32)
    (early,) = call(
        functools.partial(second_spread_early, levels),
        [spread_shape],
        half_specs,
        [state],
        8 * size,
        *(part, r1, pack, y_pack, matrices1, pack, y_pack),
    )
    pieces = call(
        functools.partial(second_spread_late, levels),
        [8 * levels] * 8,
        half_specs + [vmem(spread_shape[0], 3)],
        [state, pltpu.VMEM(*spread_shape)],
        8 * size,
        *(part, r2, pack, y_pack, matrices1, pack, y_pack, early),
    )
    received = {}
    for bits in (6, 4, 2):
        received[bits] = swap_lon(pieces[bits] + swap_lon(pieces[bits + 1], 1), bits)
    pair = swap_lon(pieces[1], 1)
    (out,) = call(
        functools.partial(finish, levels),
        [fields * levels * 8],
        [vmem((8 * levels, 128))] * 6,
        [],
        size,
        pieces[0],
        pair,
        received[2],
        received[4],
        received[6],
        matrices0,
    )
    return out.reshape(adjoint_in.shape)


def solution(mesh):
    specs = (
        P(None, None, "lat", "lon"),
        P(None, None, "lat", "lon"),
        P(None, None, "lat", "lon"),
        P(None, "lat", "lon"),
        P(None, "lat", "lon"),
        P(None, "lat", None, None),
    )

    def whole(*args):
        fields, levels, rows, points = args[0].shape
        lat, lon = mesh.shape["lat"], mesh.shape["lon"]
        ring = (fields, lon, rows // lat, points // lon) == (2, RING, 8, 128) and levels % 8 == 0 and levels * 4 == 128
        body = ring_body if ring else plain_body
        return jax.shard_map(body, mesh=mesh, in_specs=specs, out_specs=specs[0], check_vma=False)(*args)

    return whole
```

```python
import functools

import jax
import jax.numpy as jnp
from jax import lax
from jax.experimental import pallas as pl
from jax.experimental.pallas import tpu as pltpu
from jax.sharding import PartitionSpec as P

R = 2
H = 2
NODES = 4
RING = 8
LOW = H + 1
HIGH = H + 2
VMEM_LIMIT = 48 * 1024 * 1024


def shifted(array, axis, by):
    size = lax.axis_size(axis)
    return lax.ppermute(array, axis, [(i, (i + by) % size) for i in range(size)])


def from_behind(value, axis, steps):
    count = lax.axis_size(axis)
    leading, last = (max(0, -steps), min(count, count - steps))
    return lax.ppermute(value, axis, [(source, source + steps) for source in range(leading, last)])


def spread_local(carried, lat_w, lon_w, row_table, block_table, lat_start, own_block, cycle_size):
    fields, levels, lat_rows, points = carried.shape
    ext_rows = lat_rows + LOW + HIGH
    block_count = 2 * R + 3
    width = block_count * points
    rel_row = row_table - lat_start + LOW
    rel_block = (block_table - own_block + R) % cycle_size
    target = lax.broadcasted_iota(jnp.int32, (ext_rows, 4, lat_rows), 0)
    node = lax.broadcasted_iota(jnp.int32, (ext_rows, 4, lat_rows), 1)
    row_onehot = (target == rel_row[None, None, :] + node).astype(jnp.float32)
    placed_all = []
    for m in range(4):
        lon_row = jnp.zeros((fields, levels, lat_rows, points + 3), jnp.float32)
        for o in range(4):
            term = carried * (lat_w[m] * lon_w[o])[None, None]
            lon_row = lon_row + jnp.pad(term, ((0, 0), (0, 0), (0, 0), (o, 3 - o)))
        placed = jnp.zeros((fields, levels, lat_rows, width), jnp.float32)
        for d in range(2 * R + 1):
            left = (d + 1) * points - 1
            right = width - left - (points + 3)
            selected = (rel_block == d).astype(jnp.float32)[None, None, :, None]
            placed = placed + selected * jnp.pad(lon_row, ((0, 0), (0, 0), (0, 0), (left, right)))
        placed_all.append(placed)
    stacked = jnp.stack(placed_all, axis=2)
    return jnp.einsum("emj,fkmjc->fkec", row_onehot, stacked, precision=lax.Precision.HIGHEST)


def cycle_total(buffer, points):
    block_count = 2 * R + 3
    pieces = [buffer[..., q * points : (q + 1) * points] for q in range(block_count)]
    summed = pieces[R + 1]
    for q in range(block_count):
        if q != R + 1:
            summed = summed + shifted(pieces[q], "lon", q - R - 1)
    return summed


def fold_rims(buffer, lat_rows):
    upper = buffer[:, :, :LOW]
    lower = buffer[:, :, LOW + lat_rows :]
    interior = buffer[:, :, LOW : LOW + lat_rows]
    from_after = from_behind(upper, "lat", -1)
    from_before = from_behind(lower, "lat", 1)
    interior = interior + jnp.pad(from_after, ((0, 0), (0, 0), (lat_rows - LOW, 0), (0, 0)))
    interior = interior + jnp.pad(from_before, ((0, 0), (0, 0), (0, lat_rows - HIGH), (0, 0)))
    return interior


def plain_body(adjoint_in, lat_weights, lon_weights, depart_rows, depart_blocks, vertical_inverse):
    fields, levels, lat_rows, points = adjoint_in.shape
    cycle_size = lax.axis_size("lon")
    own_block = lax.axis_index("lon")
    lat_start = lax.axis_index("lat") * lat_rows
    carried = adjoint_in
    for s in (1, 0):
        partial_value = spread_local(
            carried,
            lat_weights[s],
            lon_weights[s],
            depart_rows[s, :, 0],
            depart_blocks[s, :, 0],
            lat_start,
            own_block,
            cycle_size,
        )
        gathered_rows = cycle_total(partial_value, points)
        interior = fold_rims(gathered_rows, lat_rows)
        carried = jnp.einsum(
            "imk,fmip->fkip", vertical_inverse[s], interior, precision=lax.Precision.HIGHEST
        )
    return carried


def vmem(shape, rank=2):
    return pl.BlockSpec(shape, lambda i: (0,) * rank, memory_space=pltpu.VMEM)


def call(kernel, outs, in_specs, scratch, cost, *args):
    outs = [((n, 128), jnp.float32) if isinstance(n, int) else n for n in outs]
    return pl.pallas_call(
        kernel,
        grid=(1,),
        out_shape=[jax.ShapeDtypeStruct(*out) for out in outs],
        in_specs=in_specs,
        out_specs=[vmem(shape, len(shape)) for shape, _ in outs],
        scratch_shapes=scratch,
        compiler_params=pltpu.CompilerParams(vmem_limit_bytes=VMEM_LIMIT),
        cost_estimate=pl.CostEstimate(flops=cost, bytes_accessed=cost, transcendentals=0),
    )(*args)


def even_band():
    return 1 - lax.axis_index("lat") % 2


def rolled(value):
    return [pltpu.roll(value, 127, 1), value, pltpu.roll(value, 1, 1), pltpu.roll(value, 2, 1)]


def products(weights):
    turned = rolled(weights)
    return [turned[o][0:4] * turned[o][4 + o : 5 + o] for o in range(NODES)]


def lane_masks():
    lane = lax.broadcasted_iota(jnp.int32, (8, 128), 1)
    node = lax.broadcasted_iota(jnp.int32, (8, 128), 0)
    first = jnp.maximum(node - 1, 0)
    stay = (lane >= first) & (lane < jnp.where(node == 0, 127, 128))
    return [value.astype(jnp.float32) for value in (stay, (node == 0) & (lane == 127), (node >= 2) & (lane < first))]


def masked(prods, mask, nodes):
    return [(o, prods[o] * mask[o : o + 1]) for o in nodes]


def add_terms(sources, terms, target, first):
    for m in range(NODES):
        for kk, turned in enumerate(sources):
            total = None
            for o, weight in terms:
                term = turned[o] * weight[m : m + 1]
                total = term if total is None else total + term
            target[first + m, 8 * kk : 8 * kk + 8, :] += total


def assemble(levels, rows, blocks, adj, lat_w, lon_w, v, own, other, e1, e2, *scratch):
    tables, lat_all, lon_all, v1, sems = scratch
    field, even = lax.axis_index("lon") // 4, even_band()
    per_field = 8 * levels
    sem = iter(range(7))

    def copy(source, target):
        return pltpu.make_async_copy(source, target, sems.at[next(sem)])

    small = [copy(rows, tables.at[0]), copy(blocks, tables.at[1])]
    small += [copy(lat_w, lat_all), copy(lon_w, lon_all), copy(v.at[1], v1)]
    large = []
    for out, which in ((own, field), (other, 1 - field)):
        large.append(copy(adj.at[pl.ds(pl.multiple_of(which * per_field, per_field), per_field)], out.at[pl.ds(0, per_field)]))
    for each in small + large:
        each.start()
    for each in small:
        each.wait()
    table = jnp.concatenate([tables[0], tables[1], tables[0], tables[1]], axis=0).astype(jnp.float32)
    for out in (own, other):
        out[per_field : per_field + 32, :] = lat_all[32:64, :]
        out[per_field + 32 : per_field + 64, :] = lon_all[32:64, :]
    for out, first in ((own, per_field + 64), (other, per_field + 64), (e1, 32 + levels), (e2, 32 + levels)):
        out[first : first + 8, 0:8] = table
    low = jnp.concatenate([v1[j] for j in range(4)], axis=1)
    high = jnp.concatenate([v1[j + 4] for j in range(4)], axis=1)
    for out, takes_high in ((e1, even == 1), (e2, even == 0)):
        first = jnp.where(takes_high, 4, 0)
        for i in range(4):
            out[8 * i : 8 * i + 4, :] = lat_all[pl.ds(first + i, 4, stride=8), :]
            out[8 * i + 4 : 8 * i + 8, :] = lon_all[pl.ds(first + i, 4, stride=8), :]
        out[32 : 32 + levels, :] = jnp.where(takes_high, high, low)
    for each in large:
        each.wait()


def rim_data(levels, own_tile, lat_w, lon_w, e1, e2, v, after_this, pack, matrices1, matrices0):
    even = even_band() == 1
    for i in range(8):
        pack[32 + 8 * i : 36 + 8 * i, :] = lat_w[pl.ds(i, 4, stride=8), :]
        pack[36 + 8 * i : 40 + 8 * i, :] = lon_w[pl.ds(i, 4, stride=8), :]
    pack[0:32, :] = jnp.where(even, e2[0:32, :], e1[0:32, :])
    pack[96:120, :] = jnp.where(even, e1[0:24, :], e2[0:24, :])
    tab = slice(32 + levels, 40 + levels)
    before = pltpu.roll(jnp.where(even, e2[tab, :], e1[tab, :]), 124, 1)
    after = pltpu.roll(jnp.where(even, e1[tab, :], e2[tab, :]), 12, 1)
    lane = lax.broadcasted_iota(jnp.int32, (8, 128), 1)
    pack[120:128, :] = jnp.where(lane < 4, before, jnp.where(lane < 12, pltpu.roll(own_tile[...], 4, 1), after))

    def turned(four):
        value = four.T
        high = value.astype(jnp.bfloat16).astype(jnp.float32)
        low = value - high
        return jnp.concatenate([high, low, high, low], axis=1).astype(jnp.bfloat16)

    def four(s, first):
        return jnp.concatenate([v[s, first + j] for j in range(4)], axis=1)

    at_v = slice(32, 32 + levels)
    matrices1[0 : 4 * levels, :] = turned(jnp.where(even, e2[at_v, :], e1[at_v, :]))
    matrices1[4 * levels : 8 * levels, :] = turned(four(1, 0))
    matrices1[8 * levels : 12 * levels, :] = turned(four(1, 4))
    matrices1[12 * levels : 16 * levels, :] = turned(jnp.where(even, e1[at_v, :], e2[at_v, :]))
    matrices0[0 : 4 * levels, :] = turned(four(0, 0))
    matrices0[4 * levels : 8 * levels, :] = turned(four(0, 4))


def to_scalars(sources, target, sems):
    copies = [pltpu.make_async_copy(source, target.at[n], sems.at[n]) for n, source in enumerate(sources)]
    for copy in copies:
        copy.start()
    return copies


def first_spread(levels, count, *refs):
    messages, refs = refs[:count], refs[count:]
    (*refs, masks, tables, sems) = refs
    per_field = 8 * levels
    me, lat_start = lax.axis_index("lon"), 8 * lax.axis_index("lat")
    copies = to_scalars([message.at[pl.ds(per_field + 64, 8)] for message in messages], tables, sems)
    if len(refs) == 1:
        (acc,) = refs
        acc[...] = jnp.zeros_like(acc)
    else:
        before, acc, *out = refs
        acc[...] = before[...]
    stay, back, on = lane_masks()
    for n, mask in enumerate((stay, back, jnp.zeros_like(stay), on)):
        masks[n] = mask
    for copy in copies:
        copy.wait()
    for at, message in enumerate(messages):
        for i in range(8):
            first = tables[at, 1, i].astype(jnp.int32) - lat_start + LOW
            tau = tables[at, 3, i].astype(jnp.int32)
            delta = (tau - me) & 3
            block = (tau + jnp.where(delta == 1, 7, jnp.where(delta == 3, 1, 0))) & 7
            weights = message[pl.ds(per_field + i, 8, stride=8), :]
            terms = masked(products(weights), masks[delta], range(NODES))
            sources = [rolled(message[pl.ds(8 * kk + i, 8, stride=8), :]) for kk in range(0, levels, 8)]
            add_terms(sources, terms, acc, (block // 4) * 15 + first)
    if len(refs) < 4:
        return
    even = even_band()

    def write(to, part_row, rows):
        for h in range(2):
            value = acc[h * 15 + part_row : h * 15 + part_row + rows]
            to[h * 8 * levels : (h * 8 + rows) * levels, :] = value.reshape(rows * levels, 128)

    for to, is_upper in zip(out, (even == 1, even == 0)):

        @pl.when(is_upper)
        def _(to=to):
            write(to, 7, 8)

        @pl.when(~is_upper)
        def _(to=to):
            write(to, 0, 6)


def vertical(matrix, column):
    high = column.astype(jnp.bfloat16)
    low = (column - high.astype(jnp.float32)).astype(jnp.bfloat16)
    return jnp.dot(matrix, jnp.concatenate([high, high, low, low], axis=0), preferred_element_type=jnp.float32)


def spread_half(levels, upper, part, received, own_pack, y_pack, matrices, state, tables, sems, acc):
    me, band = lax.axis_index("lon"), lax.axis_index("lat")
    lat_start, at_start, at_end = 8 * band, band == 0, band == lax.axis_size("lat") - 1
    slot = me // 4
    base = 8 * upper
    copies = to_scalars([pack.at[pl.ds(120, 8)] for pack in (own_pack, y_pack)], tables, sems)

    def exists(j):
        n = base + j
        there = (n < 15) & (~at_start | (n >= 4)) if j < 4 else n < 15
        return there & (~at_end | (n < 12)) if j >= 4 else there

    for j in range(8):
        halves = []
        for h in range(2):
            sent = received[pl.ds(pl.multiple_of((h * 8 + j - upper) * levels, levels) if j else h * 8 * levels, levels), :]
            if j == 0:
                value = jnp.where(upper == 1, part[h * 15 + 7], sent)
            else:
                value = part[h * 15 + base + j - 1] + sent
            if j == 7:
                value = jnp.where(upper == 1, 0.0, value)
            halves.append(value)
        matrix = matrices[pl.ds(pl.multiple_of((base + j) * levels, levels), levels), :]
        result = vertical(matrix, jnp.concatenate(halves, axis=1))
        state[j] = result[:, :128]
        state[8 + j] = result[:, 128:]
    for q in range(8):
        acc[q * 22 + 7 : q * 22 + 15] = jnp.zeros((8, levels, 128), jnp.float32)
    stay, back, on = lane_masks()
    for copy in copies:
        copy.wait()
    for j in range(8):
        n = base + j
        there = exists(j)
        at = pl.ds(pl.multiple_of(8 * n, 8), 8)
        for h in range(2):
            mine = slot == h
            tau = jnp.where(there, jnp.where(mine, tables[0, 2, n], tables[1, 2, n]).astype(jnp.int32), 0)
            first = jnp.where(mine, tables[0, 0, n], tables[1, 0, n]).astype(jnp.int32) - lat_start + 7
            first = jnp.where(there, first, 7)
            prods = products(jnp.where(there, jnp.where(mine, own_pack[at, :], y_pack[at, :]), 0.0))
            sources = [rolled(state[h * 8 + j, kk : kk + 8, :]) for kk in range(0, levels, 8)]
            add_terms(sources, masked(prods, stay, range(NODES)), acc, (tau ^ me) * 22 + first)
            add_terms(sources, masked(prods, back, (0,)), acc, (((tau + 7) & 7) ^ me) * 22 + first)
            add_terms(sources, masked(prods, on, (2, 3)), acc, (((tau + 1) & 7) ^ me) * 22 + first)


def second_spread_early(levels, *refs):
    (*refs, acc, state, tables, sems) = refs
    spread_half(levels, even_band(), *refs, state, tables, sems, acc)


def second_spread_late(levels, *refs):
    refs, before, outs, (state, tables, sems, acc) = refs[:5], refs[5], refs[6:14], refs[14:]
    spread_half(levels, 1 - even_band(), *refs, state, tables, sems, acc)
    for q, out in enumerate(outs):
        rows = slice(q * 22 + 7, q * 22 + 15)
        out[...] = (acc[rows] + before[rows]).reshape(8 * levels, 128)


def finish(levels, own, diagonal, across, up, pair, matrices, out):
    field = lax.axis_index("lon") // 4
    for i in range(8):
        rows = slice(i * levels, (i + 1) * levels)
        mine = own[rows, :] + pair[rows, :] + across[rows, :]
        other = up[rows, :] + diagonal[rows, :]
        result = vertical(matrices[rows, :], jnp.concatenate([mine, other], axis=1))
        for kk in range(0, levels, 8):
            out[pl.ds((field * levels + kk) * 8 + i, 8, stride=8), :] = result[kk : kk + 8, :128]
            out[pl.ds(((1 - field) * levels + kk) * 8 + i, 8, stride=8), :] = result[kk : kk + 8, 128:]


def swap_lon(value, bits):
    return lax.ppermute(value, "lon", [(i, i ^ bits) for i in range(RING)])


def swap_lat(value, odd):
    count = lax.axis_size("lat")
    pairs = [(i, i + 1) for i in range(odd, count - 1, 2)]
    return lax.ppermute(value, "lat", pairs + [(b, a) for a, b in pairs])


def ring_body(adjoint_in, lat_weights, lon_weights, depart_rows, depart_blocks, vertical_inverse):
    fields, levels, lat_rows, points = adjoint_in.shape
    per_field = 8 * levels
    size = adjoint_in.size
    message = per_field + 64 + 8
    side = 32 + levels + 8
    adjoint = adjoint_in.reshape(-1, points)
    lat_w, lon_w = lat_weights.reshape(-1, points), lon_weights.reshape(-1, points)
    sizes = [message, message, side, side]
    arguments = depart_rows[:, :, 0], depart_blocks[:, :, 0], adjoint, lat_w, lon_w, vertical_inverse
    own, other, e1, e2 = pl.pallas_call(
        functools.partial(assemble, levels),
        out_shape=[pltpu.VMEM((n, points), jnp.float32) for n in sizes],
        in_specs=[pl.BlockSpec(memory_space=pltpu.HBM)] * 6,
        out_specs=[pl.BlockSpec(memory_space=pltpu.VMEM)] * 4,
        scratch_shapes=[
            pltpu.VMEM((2, 2, 8), jnp.int32),
            pltpu.VMEM((64, points), jnp.float32),
            pltpu.VMEM((64, points), jnp.float32),
            pltpu.VMEM((8, levels, levels), jnp.float32),
            pltpu.SemaphoreType.DMA((7,)),
        ],
        compiler_params=pltpu.CompilerParams(vmem_limit_bytes=VMEM_LIMIT),
    )(*(pltpu.with_memory_space_constraint(value, pltpu.HBM) for value in arguments))
    far = {2: swap_lon(own, 2), 4: swap_lon(other, 4), 6: swap_lon(other, 6)}
    tile = pl.BlockSpec((8, 128), lambda i: (message // 8 - 1, 0), memory_space=pltpu.VMEM)
    e1, e2 = swap_lat(e1, 0), swap_lat(e2, 1)
    partial = ((30, levels, 128), jnp.float32)

    def spread(those, *before, outs=()):
        count = len(those)
        scratch = [pltpu.VMEM((4, 8, 128), jnp.float32), pltpu.SMEM((count, 8, 128), jnp.float32)]
        return call(
            functools.partial(first_spread, levels, count),
            [partial, *outs],
            [vmem((message, 128))] * count + [vmem(partial[0], 3)] * len(before),
            scratch + [pltpu.SemaphoreType.DMA((count,))],
            4 * size,
            *those,
            *before,
        )

    (part,) = spread([own])
    far[4], part, e1 = lax.optimization_barrier((far[4], part, e1))
    far[6], e2 = lax.optimization_barrier((far[6], e2))
    (part,) = spread([far[4], far[6], far[2]], part)
    others = [swap_lon(value, 1) for value in (own, far[4], far[6], far[2])]
    part, m1, m2 = spread(others, part, outs=(16 * levels, 16 * levels))
    r1, r2 = swap_lat(m1, 0), swap_lat(m2, 1)
    pack, matrices1, matrices0 = call(
        functools.partial(rim_data, levels),
        [128, ((16 * levels, 128), jnp.bfloat16), ((8 * levels, 128), jnp.bfloat16)],
        [tile, vmem((64, 128)), vmem((64, 128)), vmem((side, 128)), vmem((side, 128))]
        + [vmem(vertical_inverse.shape, 4), vmem((8, levels, 128), 3)],
        [],
        size,
        own,
        lat_w,
        lon_w,
        e1,
        e2,
        vertical_inverse,
        part,
    )
    y_pack = swap_lon(pack, 4)
    half_specs = [vmem(partial[0], 3), vmem((16 * levels, 128)), vmem((128, 128)), vmem((128, 128))]
    half_specs += [vmem((16 * levels, 128))]
    spread_shape = ((8 * 22, levels, 128), jnp.float32)
    scratch = [pltpu.VMEM((16, levels, 128), jnp.float32), pltpu.SMEM((2, 8, 128), jnp.float32), pltpu.SemaphoreType.DMA((2,))]
    (early,) = call(
        functools.partial(second_spread_early, levels),
        [spread_shape],
        half_specs,
        scratch,
        8 * size,
        *(part, r1, pack, y_pack, matrices1),
    )
    pieces = call(
        functools.partial(second_spread_late, levels),
        [8 * levels] * 8,
        half_specs + [vmem(spread_shape[0], 3)],
        scratch + [pltpu.VMEM(*spread_shape)],
        8 * size,
        *(part, r2, pack, y_pack, matrices1, early),
    )
    received = {}
    for bits in (6, 4, 2):
        received[bits] = swap_lon(pieces[bits] + swap_lon(pieces[bits + 1], 1), bits)
    pair = swap_lon(pieces[1], 1)
    (out,) = call(
        functools.partial(finish, levels),
        [fields * levels * 8],
        [vmem((8 * levels, 128))] * 6,
        [],
        size,
        pieces[0],
        received[6],
        received[2],
        received[4],
        pair,
        matrices0,
    )
    return out.reshape(adjoint_in.shape)


def solution(mesh):
    specs = (
        P(None, None, "lat", "lon"),
        P(None, None, "lat", "lon"),
        P(None, None, "lat", "lon"),
        P(None, "lat", "lon"),
        P(None, "lat", "lon"),
        P(None, "lat", None, None),
    )

    def whole(*args):
        fields, levels, rows, points = args[0].shape
        lat, lon = mesh.shape["lat"], mesh.shape["lon"]
        ring = (fields, lon, rows // lat, points // lon) == (2, RING, 8, 128) and levels % 8 == 0 and levels * 4 == 128
        body = ring_body if ring else plain_body
        return jax.shard_map(body, mesh=mesh, in_specs=specs, out_specs=specs[0], check_vma=False)(*args)

    return whole
```

```python
import functools

import jax
import jax.numpy as jnp
from jax import lax
from jax.experimental import pallas as pl
from jax.experimental.pallas import tpu as pltpu
from jax.sharding import PartitionSpec as P

R = 2
H = 2
NODES = 4
RING = 8
LOW = H + 1
HIGH = H + 2
VMEM_LIMIT = 48 * 1024 * 1024


def shifted(array, axis, by):
    size = lax.axis_size(axis)
    return lax.ppermute(array, axis, [(i, (i + by) % size) for i in range(size)])


def from_behind(value, axis, steps):
    count = lax.axis_size(axis)
    leading, last = (max(0, -steps), min(count, count - steps))
    return lax.ppermute(value, axis, [(source, source + steps) for source in range(leading, last)])


def spread_local(carried, lat_w, lon_w, row_table, block_table, lat_start, own_block, cycle_size):
    fields, levels, lat_rows, points = carried.shape
    ext_rows = lat_rows + LOW + HIGH
    block_count = 2 * R + 3
    width = block_count * points
    rel_row = row_table - lat_start + LOW
    rel_block = (block_table - own_block + R) % cycle_size
    target = lax.broadcasted_iota(jnp.int32, (ext_rows, 4, lat_rows), 0)
    node = lax.broadcasted_iota(jnp.int32, (ext_rows, 4, lat_rows), 1)
    row_onehot = (target == rel_row[None, None, :] + node).astype(jnp.float32)
    placed_all = []
    for m in range(4):
        lon_row = jnp.zeros((fields, levels, lat_rows, points + 3), jnp.float32)
        for o in range(4):
            term = carried * (lat_w[m] * lon_w[o])[None, None]
            lon_row = lon_row + jnp.pad(term, ((0, 0), (0, 0), (0, 0), (o, 3 - o)))
        placed = jnp.zeros((fields, levels, lat_rows, width), jnp.float32)
        for d in range(2 * R + 1):
            left = (d + 1) * points - 1
            right = width - left - (points + 3)
            selected = (rel_block == d).astype(jnp.float32)[None, None, :, None]
            placed = placed + selected * jnp.pad(lon_row, ((0, 0), (0, 0), (0, 0), (left, right)))
        placed_all.append(placed)
    stacked = jnp.stack(placed_all, axis=2)
    return jnp.einsum("emj,fkmjc->fkec", row_onehot, stacked, precision=lax.Precision.HIGHEST)


def cycle_total(buffer, points):
    block_count = 2 * R + 3
    pieces = [buffer[..., q * points : (q + 1) * points] for q in range(block_count)]
    summed = pieces[R + 1]
    for q in range(block_count):
        if q != R + 1:
            summed = summed + shifted(pieces[q], "lon", q - R - 1)
    return summed


def fold_rims(buffer, lat_rows):
    upper = buffer[:, :, :LOW]
    lower = buffer[:, :, LOW + lat_rows :]
    interior = buffer[:, :, LOW : LOW + lat_rows]
    from_after = from_behind(upper, "lat", -1)
    from_before = from_behind(lower, "lat", 1)
    interior = interior + jnp.pad(from_after, ((0, 0), (0, 0), (lat_rows - LOW, 0), (0, 0)))
    interior = interior + jnp.pad(from_before, ((0, 0), (0, 0), (0, lat_rows - HIGH), (0, 0)))
    return interior


def plain_body(adjoint_in, lat_weights, lon_weights, depart_rows, depart_blocks, vertical_inverse):
    fields, levels, lat_rows, points = adjoint_in.shape
    cycle_size = lax.axis_size("lon")
    own_block = lax.axis_index("lon")
    lat_start = lax.axis_index("lat") * lat_rows
    carried = adjoint_in
    for s in (1, 0):
        partial_value = spread_local(
            carried,
            lat_weights[s],
            lon_weights[s],
            depart_rows[s, :, 0],
            depart_blocks[s, :, 0],
            lat_start,
            own_block,
            cycle_size,
        )
        gathered_rows = cycle_total(partial_value, points)
        interior = fold_rims(gathered_rows, lat_rows)
        carried = jnp.einsum(
            "imk,fmip->fkip", vertical_inverse[s], interior, precision=lax.Precision.HIGHEST
        )
    return carried


def vmem(shape, rank=2):
    return pl.BlockSpec(shape, lambda i: (0,) * rank, memory_space=pltpu.VMEM)


def call(kernel, outs, in_specs, scratch, cost, *args):
    outs = [((n, 128), jnp.float32) if isinstance(n, int) else n for n in outs]
    return pl.pallas_call(
        kernel,
        grid=(1,),
        out_shape=[jax.ShapeDtypeStruct(*out) for out in outs],
        in_specs=in_specs,
        out_specs=[vmem(shape, len(shape)) for shape, _ in outs],
        scratch_shapes=scratch,
        compiler_params=pltpu.CompilerParams(vmem_limit_bytes=VMEM_LIMIT),
        cost_estimate=pl.CostEstimate(flops=cost, bytes_accessed=cost, transcendentals=0),
    )(*args)


def even_band():
    return 1 - lax.axis_index("lat") % 2


def rolled(value):
    return [pltpu.roll(value, 127, 1), value, pltpu.roll(value, 1, 1), pltpu.roll(value, 2, 1)]


def products(weights):
    turned = rolled(weights)
    return [turned[o][0:4] * turned[o][4 + o : 5 + o] for o in range(NODES)]


def lane_masks():
    lane = lax.broadcasted_iota(jnp.int32, (8, 128), 1)
    node = lax.broadcasted_iota(jnp.int32, (8, 128), 0)
    first = jnp.maximum(node - 1, 0)
    stay = (lane >= first) & (lane < jnp.where(node == 0, 127, 128))
    return [value.astype(jnp.float32) for value in (stay, (node == 0) & (lane == 127), (node >= 2) & (lane < first))]


def masked(prods, mask, nodes):
    return [(o, prods[o] * mask[o : o + 1]) for o in nodes]


def add_terms(sources, terms, target, first):
    for m in range(NODES):
        for kk, turned in enumerate(sources):
            total = None
            for o, weight in terms:
                term = turned[o] * weight[m : m + 1]
                total = term if total is None else total + term
            target[first + m, 8 * kk : 8 * kk + 8, :] += total


def assemble(levels, rows, blocks, adj, lat_w, lon_w, v, own, other, e1, e2, lat_all, lon_all, v_all, tables, sems):
    field, even = lax.axis_index("lon") // 4, even_band()
    per_field = 8 * levels
    sem = iter(range(7))

    def copy(source, target):
        return pltpu.make_async_copy(source, target, sems.at[next(sem)])

    small = [copy(rows, tables.at[0]), copy(blocks, tables.at[1])]
    small += [copy(lat_w, lat_all), copy(lon_w, lon_all), copy(v, v_all)]
    large = []
    for out, which in ((own, field), (other, 1 - field)):
        large.append(copy(adj.at[pl.ds(pl.multiple_of(which * per_field, per_field), per_field)], out.at[pl.ds(0, per_field)]))
    for each in small + large:
        each.start()
    for each in small:
        each.wait()
    table = jnp.concatenate([tables[0], tables[1], tables[0], tables[1]], axis=0).astype(jnp.float32)
    for out in (own, other):
        out[per_field : per_field + 32, :] = lat_all[32:64, :]
        out[per_field + 32 : per_field + 64, :] = lon_all[32:64, :]
    for out, first in ((own, per_field + 64), (other, per_field + 64), (e1, 32 + levels), (e2, 32 + levels)):
        out[first : first + 8, 0:8] = table
    low = jnp.concatenate([v_all[1, j] for j in range(4)], axis=1)
    high = jnp.concatenate([v_all[1, j + 4] for j in range(4)], axis=1)
    for out, takes_high in ((e1, even == 1), (e2, even == 0)):
        first = jnp.where(takes_high, 4, 0)
        for i in range(4):
            out[8 * i : 8 * i + 4, :] = lat_all[pl.ds(first + i, 4, stride=8), :]
            out[8 * i + 4 : 8 * i + 8, :] = lon_all[pl.ds(first + i, 4, stride=8), :]
        out[32 : 32 + levels, :] = jnp.where(takes_high, high, low)
    for each in large:
        each.wait()


def rim_data(levels, own_tile, lat_w, lon_w, e1, e2, v, after_this, pack, matrices1, matrices0):
    even = even_band() == 1
    for i in range(8):
        pack[32 + 8 * i : 36 + 8 * i, :] = lat_w[pl.ds(i, 4, stride=8), :]
        pack[36 + 8 * i : 40 + 8 * i, :] = lon_w[pl.ds(i, 4, stride=8), :]
    pack[0:32, :] = jnp.where(even, e2[0:32, :], e1[0:32, :])
    pack[96:120, :] = jnp.where(even, e1[0:24, :], e2[0:24, :])
    tab = slice(32 + levels, 40 + levels)
    before = pltpu.roll(jnp.where(even, e2[tab, :], e1[tab, :]), 124, 1)
    after = pltpu.roll(jnp.where(even, e1[tab, :], e2[tab, :]), 12, 1)
    lane = lax.broadcasted_iota(jnp.int32, (8, 128), 1)
    pack[120:128, :] = jnp.where(lane < 4, before, jnp.where(lane < 12, pltpu.roll(own_tile[...], 4, 1), after))

    def turned(four):
        value = four.T
        high = value.astype(jnp.bfloat16).astype(jnp.float32)
        low = value - high
        return jnp.concatenate([high, low, high, low], axis=1).astype(jnp.bfloat16)

    def four(s, first):
        return jnp.concatenate([v[s, first + j] for j in range(4)], axis=1)

    at_v = slice(32, 32 + levels)
    matrices1[0 : 4 * levels, :] = turned(jnp.where(even, e2[at_v, :], e1[at_v, :]))
    matrices1[4 * levels : 8 * levels, :] = turned(four(1, 0))
    matrices1[8 * levels : 12 * levels, :] = turned(four(1, 4))
    matrices1[12 * levels : 16 * levels, :] = turned(jnp.where(even, e1[at_v, :], e2[at_v, :]))
    matrices0[0 : 4 * levels, :] = turned(four(0, 0))
    matrices0[4 * levels : 8 * levels, :] = turned(four(0, 4))


def to_scalars(sources, target, sems):
    copies = [pltpu.make_async_copy(source, target.at[n], sems.at[n]) for n, source in enumerate(sources)]
    for copy in copies:
        copy.start()
    return copies


def first_spread(levels, count, *refs):
    messages, refs = refs[:count], refs[count:]
    (*refs, masks, tables, sems) = refs
    per_field = 8 * levels
    me, lat_start = lax.axis_index("lon"), 8 * lax.axis_index("lat")
    copies = to_scalars([message.at[pl.ds(per_field + 64, 8)] for message in messages], tables, sems)
    if len(refs) == 1:
        (acc,) = refs
        acc[...] = jnp.zeros_like(acc)
    else:
        before, acc, *out = refs
        acc[...] = before[...]
    stay, back, on = lane_masks()
    for n, mask in enumerate((stay, back, jnp.zeros_like(stay), on)):
        masks[n] = mask
    for copy in copies:
        copy.wait()
    for at, message in enumerate(messages):
        for i in range(8):
            first = tables[at, 1, i].astype(jnp.int32) - lat_start + LOW
            tau = tables[at, 3, i].astype(jnp.int32)
            delta = (tau - me) & 3
            block = (tau + jnp.where(delta == 1, 7, jnp.where(delta == 3, 1, 0))) & 7
            weights = message[pl.ds(per_field + i, 8, stride=8), :]
            terms = masked(products(weights), masks[delta], range(NODES))
            sources = [rolled(message[pl.ds(8 * kk + i, 8, stride=8), :]) for kk in range(0, levels, 8)]
            add_terms(sources, terms, acc, (block // 4) * 15 + first)
    if len(refs) < 4:
        return
    even = even_band()

    def write(to, part_row, rows):
        for h in range(2):
            value = acc[h * 15 + part_row : h * 15 + part_row + rows]
            to[h * 8 * levels : (h * 8 + rows) * levels, :] = value.reshape(rows * levels, 128)

    for to, is_upper in zip(out, (even == 1, even == 0)):

        @pl.when(is_upper)
        def _(to=to):
            write(to, 7, 8)

        @pl.when(~is_upper)
        def _(to=to):
            write(to, 0, 6)


def vertical(matrix, column):
    high = column.astype(jnp.bfloat16)
    low = (column - high.astype(jnp.float32)).astype(jnp.bfloat16)
    return jnp.dot(matrix, jnp.concatenate([high, high, low, low], axis=0), preferred_element_type=jnp.float32)


def spread_half(levels, upper, part, received, own_pack, y_pack, matrices, state, tables, sems, acc):
    me, band = lax.axis_index("lon"), lax.axis_index("lat")
    lat_start, at_start, at_end = 8 * band, band == 0, band == lax.axis_size("lat") - 1
    slot = me // 4
    base = 8 * upper
    copies = to_scalars([pack.at[pl.ds(120, 8)] for pack in (own_pack, y_pack)], tables, sems)

    def exists(j):
        n = base + j
        there = (n < 15) & (~at_start | (n >= 4)) if j < 4 else n < 15
        return there & (~at_end | (n < 12)) if j >= 4 else there

    sender = jnp.where(upper == 1, ~at_end, ~at_start)
    for j in range(8):
        halves = []
        for h in range(2):
            sent = received[pl.ds(pl.multiple_of((h * 8 + j - upper) * levels, levels) if j else h * 8 * levels, levels), :]
            sent = jnp.where(sender, sent, 0.0)
            if j == 0:
                value = jnp.where(upper == 1, part[h * 15 + 7], sent)
            else:
                value = part[h * 15 + base + j - 1] + sent
            if j == 7:
                value = jnp.where(upper == 1, 0.0, value)
            halves.append(value)
        matrix = matrices[pl.ds(pl.multiple_of((base + j) * levels, levels), levels), :]
        result = vertical(matrix, jnp.concatenate(halves, axis=1))
        state[j] = result[:, :128]
        state[8 + j] = result[:, 128:]
    for q in range(8):
        acc[q * 22 + 7 : q * 22 + 15] = jnp.zeros((8, levels, 128), jnp.float32)
    stay, back, on = lane_masks()
    for copy in copies:
        copy.wait()
    for j in range(8):
        n = base + j
        there = exists(j)
        at = pl.ds(pl.multiple_of(8 * n, 8), 8)
        for h in range(2):
            mine = slot == h
            tau = jnp.where(there, jnp.where(mine, tables[0, 2, n], tables[1, 2, n]).astype(jnp.int32), 0)
            first = jnp.where(mine, tables[0, 0, n], tables[1, 0, n]).astype(jnp.int32) - lat_start + 7
            first = jnp.where(there, first, 7)
            prods = products(jnp.where(there, jnp.where(mine, own_pack[at, :], y_pack[at, :]), 0.0))
            sources = [rolled(state[h * 8 + j, kk : kk + 8, :]) for kk in range(0, levels, 8)]
            add_terms(sources, masked(prods, stay, range(NODES)), acc, (tau ^ me) * 22 + first)
            add_terms(sources, masked(prods, back, (0,)), acc, (((tau + 7) & 7) ^ me) * 22 + first)
            add_terms(sources, masked(prods, on, (2, 3)), acc, (((tau + 1) & 7) ^ me) * 22 + first)


def second_spread_early(levels, *refs):
    (*refs, acc, state, tables, sems) = refs
    spread_half(levels, even_band(), *refs, state, tables, sems, acc)


def second_spread_late(levels, *refs):
    refs, before, outs, (state, tables, sems, acc) = refs[:5], refs[5], refs[6:14], refs[14:]
    spread_half(levels, 1 - even_band(), *refs, state, tables, sems, acc)
    for q, out in enumerate(outs):
        rows = slice(q * 22 + 7, q * 22 + 15)
        out[...] = (acc[rows] + before[rows]).reshape(8 * levels, 128)


def finish(levels, own, diagonal, across, up, pair, matrices, out):
    field = lax.axis_index("lon") // 4
    for i in range(8):
        rows = slice(i * levels, (i + 1) * levels)
        mine = own[rows, :] + pair[rows, :] + across[rows, :]
        other = up[rows, :] + diagonal[rows, :]
        result = vertical(matrices[rows, :], jnp.concatenate([mine, other], axis=1))
        for kk in range(0, levels, 8):
            out[pl.ds((field * levels + kk) * 8 + i, 8, stride=8), :] = result[kk : kk + 8, :128]
            out[pl.ds(((1 - field) * levels + kk) * 8 + i, 8, stride=8), :] = result[kk : kk + 8, 128:]


def swap_lon(value, bits):
    return lax.ppermute(value, "lon", [(i, i ^ bits) for i in range(RING)])


def swap_lat(value, odd):
    count = lax.axis_size("lat")
    pairs = [(i, i + 1) for i in range(odd, count - 1, 2)]
    partner = {a: b for pair in pairs for a, b in (pair, pair[::-1])}
    moves = [(i * RING + j, partner[i] * RING + j if i in partner else i * RING + (j ^ 1)) for i in range(count) for j in range(RING)]
    return lax.ppermute(value, ("lat", "lon"), moves)


def ring_body(adjoint_in, lat_weights, lon_weights, depart_rows, depart_blocks, vertical_inverse):
    fields, levels, lat_rows, points = adjoint_in.shape
    per_field = 8 * levels
    size = adjoint_in.size
    message = per_field + 64 + 8
    side = 32 + levels + 8
    adjoint = adjoint_in.reshape(-1, points)
    lat_w, lon_w = lat_weights.reshape(-1, points), lon_weights.reshape(-1, points)
    shapes = [(n, points) for n in (message, message, side, side, 64, 64)] + [vertical_inverse.shape]
    arguments = depart_rows[:, :, 0], depart_blocks[:, :, 0], adjoint, lat_w, lon_w, vertical_inverse
    own, other, e1, e2, lat_w, lon_w, matrices = pl.pallas_call(
        functools.partial(assemble, levels),
        out_shape=[pltpu.VMEM(shape, jnp.float32) for shape in shapes],
        in_specs=[pl.BlockSpec(memory_space=pltpu.HBM)] * 6,
        out_specs=[pl.BlockSpec(memory_space=pltpu.VMEM)] * 7,
        scratch_shapes=[pltpu.VMEM((2, 2, 8), jnp.int32), pltpu.SemaphoreType.DMA((7,))],
        compiler_params=pltpu.CompilerParams(vmem_limit_bytes=VMEM_LIMIT),
    )(*(pltpu.with_memory_space_constraint(value, pltpu.HBM) for value in arguments))
    far = {2: swap_lon(own, 2), 4: swap_lon(other, 4), 6: swap_lon(other, 6)}
    tile = pl.BlockSpec((8, 128), lambda i: (message // 8 - 1, 0), memory_space=pltpu.VMEM)
    e1, e2 = swap_lat(e1, 0), swap_lat(e2, 1)
    partial = ((30, levels, 128), jnp.float32)

    def spread(those, *before, outs=()):
        count = len(those)
        scratch = [pltpu.VMEM((4, 8, 128), jnp.float32), pltpu.SMEM((count, 8, 128), jnp.float32)]
        return call(
            functools.partial(first_spread, levels, count),
            [partial, *outs],
            [vmem((message, 128))] * count + [vmem(partial[0], 3)] * len(before),
            scratch + [pltpu.SemaphoreType.DMA((count,))],
            4 * size,
            *those,
            *before,
        )

    (part,) = spread([own])
    far[4], part, e1 = lax.optimization_barrier((far[4], part, e1))
    far[6], e2 = lax.optimization_barrier((far[6], e2))
    (part,) = spread([far[4], far[6], far[2]], part)
    others = [swap_lon(value, 1) for value in (own, far[4], far[6], far[2])]
    part, m1, m2 = spread(others, part, outs=(16 * levels, 16 * levels))
    r1, r2 = swap_lat(m1, 0), swap_lat(m2, 1)
    pack, matrices1, matrices0 = call(
        functools.partial(rim_data, levels),
        [128, ((16 * levels, 128), jnp.bfloat16), ((8 * levels, 128), jnp.bfloat16)],
        [tile, vmem((64, 128)), vmem((64, 128)), vmem((side, 128)), vmem((side, 128))]
        + [vmem(vertical_inverse.shape, 4), vmem((8, levels, 128), 3)],
        [],
        size,
        own,
        lat_w,
        lon_w,
        e1,
        e2,
        matrices,
        part,
    )
    y_pack = swap_lon(pack, 4)
    half_specs = [vmem(partial[0], 3), vmem((16 * levels, 128)), vmem((128, 128)), vmem((128, 128))]
    half_specs += [vmem((16 * levels, 128))]
    spread_shape = ((8 * 22, levels, 128), jnp.float32)
    scratch = [pltpu.VMEM((16, levels, 128), jnp.float32), pltpu.SMEM((2, 8, 128), jnp.float32), pltpu.SemaphoreType.DMA((2,))]
    (early,) = call(
        functools.partial(second_spread_early, levels),
        [spread_shape],
        half_specs,
        scratch,
        8 * size,
        *(part, r1, pack, y_pack, matrices1),
    )
    pieces = call(
        functools.partial(second_spread_late, levels),
        [8 * levels] * 8,
        half_specs + [vmem(spread_shape[0], 3)],
        scratch + [pltpu.VMEM(*spread_shape)],
        8 * size,
        *(part, r2, pack, y_pack, matrices1, early),
    )
    received = {}
    for bits in (6, 4, 2):
        received[bits] = swap_lon(pieces[bits] + swap_lon(pieces[bits + 1], 1), bits)
    pair = swap_lon(pieces[1], 1)
    (out,) = call(
        functools.partial(finish, levels),
        [fields * levels * 8],
        [vmem((8 * levels, 128))] * 6,
        [],
        size,
        pieces[0],
        received[6],
        received[2],
        received[4],
        pair,
        matrices0,
    )
    return out.reshape(adjoint_in.shape)


def solution(mesh):
    specs = (
        P(None, None, "lat", "lon"),
        P(None, None, "lat", "lon"),
        P(None, None, "lat", "lon"),
        P(None, "lat", "lon"),
        P(None, "lat", "lon"),
        P(None, "lat", None, None),
    )

    def whole(*args):
        fields, levels, rows, points = args[0].shape
        lat, lon = mesh.shape["lat"], mesh.shape["lon"]
        ring = (fields, lon, rows // lat, points // lon) == (2, RING, 8, 128) and levels % 8 == 0 and levels * 4 == 128
        body = ring_body if ring else plain_body
        return jax.shard_map(body, mesh=mesh, in_specs=specs, out_specs=specs[0], check_vma=False)(*args)

    return whole
```

```python
import functools

import jax
import jax.numpy as jnp
from jax import lax
from jax.experimental import pallas as pl
from jax.experimental.pallas import tpu as pltpu
from jax.sharding import PartitionSpec as P

R = 2
H = 2
NODES = 4
RING = 8
LOW = H + 1
HIGH = H + 2
VMEM_LIMIT = 48 * 1024 * 1024


def shifted(array, axis, by):
    size = lax.axis_size(axis)
    return lax.ppermute(array, axis, [(i, (i + by) % size) for i in range(size)])


def from_behind(value, axis, steps):
    count = lax.axis_size(axis)
    leading, last = (max(0, -steps), min(count, count - steps))
    return lax.ppermute(value, axis, [(source, source + steps) for source in range(leading, last)])


def spread_local(carried, lat_w, lon_w, row_table, block_table, lat_start, own_block, cycle_size):
    fields, levels, lat_rows, points = carried.shape
    ext_rows = lat_rows + LOW + HIGH
    block_count = 2 * R + 3
    width = block_count * points
    rel_row = row_table - lat_start + LOW
    rel_block = (block_table - own_block + R) % cycle_size
    target = lax.broadcasted_iota(jnp.int32, (ext_rows, 4, lat_rows), 0)
    node = lax.broadcasted_iota(jnp.int32, (ext_rows, 4, lat_rows), 1)
    row_onehot = (target == rel_row[None, None, :] + node).astype(jnp.float32)
    placed_all = []
    for m in range(4):
        lon_row = jnp.zeros((fields, levels, lat_rows, points + 3), jnp.float32)
        for o in range(4):
            term = carried * (lat_w[m] * lon_w[o])[None, None]
            lon_row = lon_row + jnp.pad(term, ((0, 0), (0, 0), (0, 0), (o, 3 - o)))
        placed = jnp.zeros((fields, levels, lat_rows, width), jnp.float32)
        for d in range(2 * R + 1):
            left = (d + 1) * points - 1
            right = width - left - (points + 3)
            selected = (rel_block == d).astype(jnp.float32)[None, None, :, None]
            placed = placed + selected * jnp.pad(lon_row, ((0, 0), (0, 0), (0, 0), (left, right)))
        placed_all.append(placed)
    stacked = jnp.stack(placed_all, axis=2)
    return jnp.einsum("emj,fkmjc->fkec", row_onehot, stacked, precision=lax.Precision.HIGHEST)


def cycle_total(buffer, points):
    block_count = 2 * R + 3
    pieces = [buffer[..., q * points : (q + 1) * points] for q in range(block_count)]
    summed = pieces[R + 1]
    for q in range(block_count):
        if q != R + 1:
            summed = summed + shifted(pieces[q], "lon", q - R - 1)
    return summed


def fold_rims(buffer, lat_rows):
    upper = buffer[:, :, :LOW]
    lower = buffer[:, :, LOW + lat_rows :]
    interior = buffer[:, :, LOW : LOW + lat_rows]
    from_after = from_behind(upper, "lat", -1)
    from_before = from_behind(lower, "lat", 1)
    interior = interior + jnp.pad(from_after, ((0, 0), (0, 0), (lat_rows - LOW, 0), (0, 0)))
    interior = interior + jnp.pad(from_before, ((0, 0), (0, 0), (0, lat_rows - HIGH), (0, 0)))
    return interior


def plain_body(adjoint_in, lat_weights, lon_weights, depart_rows, depart_blocks, vertical_inverse):
    fields, levels, lat_rows, points = adjoint_in.shape
    cycle_size = lax.axis_size("lon")
    own_block = lax.axis_index("lon")
    lat_start = lax.axis_index("lat") * lat_rows
    carried = adjoint_in
    for s in (1, 0):
        partial_value = spread_local(
            carried,
            lat_weights[s],
            lon_weights[s],
            depart_rows[s, :, 0],
            depart_blocks[s, :, 0],
            lat_start,
            own_block,
            cycle_size,
        )
        gathered_rows = cycle_total(partial_value, points)
        interior = fold_rims(gathered_rows, lat_rows)
        carried = jnp.einsum(
            "imk,fmip->fkip", vertical_inverse[s], interior, precision=lax.Precision.HIGHEST
        )
    return carried


def vmem(shape, rank=2):
    return pl.BlockSpec(shape, lambda i: (0,) * rank, memory_space=pltpu.VMEM)


def call(kernel, outs, in_specs, scratch, cost, *args):
    outs = [((n, 128), jnp.float32) if isinstance(n, int) else n for n in outs]
    return pl.pallas_call(
        kernel,
        grid=(1,),
        out_shape=[jax.ShapeDtypeStruct(*out) for out in outs],
        in_specs=in_specs,
        out_specs=[vmem(shape, len(shape)) for shape, _ in outs],
        scratch_shapes=scratch,
        compiler_params=pltpu.CompilerParams(vmem_limit_bytes=VMEM_LIMIT),
        cost_estimate=pl.CostEstimate(flops=cost, bytes_accessed=cost, transcendentals=0),
    )(*args)


def even_band():
    return 1 - lax.axis_index("lat") % 2


def rolled(value):
    return [pltpu.roll(value, 127, 1), value, pltpu.roll(value, 1, 1), pltpu.roll(value, 2, 1)]


def products(weights):
    turned = rolled(weights)
    return [turned[o][0:4] * turned[o][4 + o : 5 + o] for o in range(NODES)]


def lane_masks():
    lane = lax.broadcasted_iota(jnp.int32, (8, 128), 1)
    node = lax.broadcasted_iota(jnp.int32, (8, 128), 0)
    first = jnp.maximum(node - 1, 0)
    stay = (lane >= first) & (lane < jnp.where(node == 0, 127, 128))
    return [value.astype(jnp.float32) for value in (stay, (node == 0) & (lane == 127), (node >= 2) & (lane < first))]


def masked(prods, mask, nodes):
    return [(o, prods[o] * mask[o : o + 1]) for o in nodes]


def add_terms(sources, terms, target, first):
    for m in range(NODES):
        for kk, turned in enumerate(sources):
            total = None
            for o, weight in terms:
                term = turned[o] * weight[m : m + 1]
                total = term if total is None else total + term
            target[first + m, 8 * kk : 8 * kk + 8, :] += total


def assemble(levels, rows, blocks, adj, lat_w, lon_w, v, own, other, e1, e2, lat_all, lon_all, v_all, tables, sems):
    field, even = lax.axis_index("lon") // 4, even_band()
    per_field = 8 * levels
    sem = iter(range(7))

    def copy(source, target):
        return pltpu.make_async_copy(source, target, sems.at[next(sem)])

    small = [copy(rows, tables.at[0]), copy(blocks, tables.at[1])]
    small += [copy(lat_w, lat_all), copy(lon_w, lon_all), copy(v, v_all)]
    large = []
    for out, which in ((own, field), (other, 1 - field)):
        large.append(copy(adj.at[pl.ds(pl.multiple_of(which * per_field, per_field), per_field)], out.at[pl.ds(0, per_field)]))
    for each in small + large:
        each.start()
    for each in small:
        each.wait()
    table = jnp.concatenate([tables[0], tables[1], tables[0], tables[1]], axis=0).astype(jnp.float32)
    for out in (own, other):
        out[per_field : per_field + 32, :] = lat_all[32:64, :]
        out[per_field + 32 : per_field + 64, :] = lon_all[32:64, :]
    for out, first in ((own, per_field + 64), (other, per_field + 64), (e1, 32 + levels), (e2, 32 + levels)):
        out[first : first + 8, 0:8] = table
    low = jnp.concatenate([v_all[1, j] for j in range(4)], axis=1)
    high = jnp.concatenate([v_all[1, j + 4] for j in range(4)], axis=1)
    for out, takes_high in ((e1, even == 1), (e2, even == 0)):
        first = jnp.where(takes_high, 4, 0)
        for i in range(4):
            out[8 * i : 8 * i + 4, :] = lat_all[pl.ds(first + i, 4, stride=8), :]
            out[8 * i + 4 : 8 * i + 8, :] = lon_all[pl.ds(first + i, 4, stride=8), :]
        out[32 : 32 + levels, :] = jnp.where(takes_high, high, low)
    for each in large:
        each.wait()


def rim_data(levels, own_tile, lat_w, lon_w, e1, e2, v, after_this, pack, matrices1, matrices0):
    even = even_band() == 1
    for i in range(8):
        pack[32 + 8 * i : 36 + 8 * i, :] = lat_w[pl.ds(i, 4, stride=8), :]
        pack[36 + 8 * i : 40 + 8 * i, :] = lon_w[pl.ds(i, 4, stride=8), :]
    pack[0:32, :] = jnp.where(even, e2[0:32, :], e1[0:32, :])
    pack[96:120, :] = jnp.where(even, e1[0:24, :], e2[0:24, :])
    tab = slice(32 + levels, 40 + levels)
    before = pltpu.roll(jnp.where(even, e2[tab, :], e1[tab, :]), 124, 1)
    after = pltpu.roll(jnp.where(even, e1[tab, :], e2[tab, :]), 12, 1)
    lane = lax.broadcasted_iota(jnp.int32, (8, 128), 1)
    pack[120:128, :] = jnp.where(lane < 4, before, jnp.where(lane < 12, pltpu.roll(own_tile[...], 4, 1), after))

    def turned(four):
        value = four.T
        high = value.astype(jnp.bfloat16).astype(jnp.float32)
        low = value - high
        return jnp.concatenate([high, low, high, low], axis=1).astype(jnp.bfloat16)

    def four(s, first):
        return jnp.concatenate([v[s, first + j] for j in range(4)], axis=1)

    at_v = slice(32, 32 + levels)
    matrices1[0 : 4 * levels, :] = turned(jnp.where(even, e2[at_v, :], e1[at_v, :]))
    matrices1[4 * levels : 8 * levels, :] = turned(four(1, 0))
    matrices1[8 * levels : 12 * levels, :] = turned(four(1, 4))
    matrices1[12 * levels : 16 * levels, :] = turned(jnp.where(even, e1[at_v, :], e2[at_v, :]))
    matrices0[0 : 4 * levels, :] = turned(four(0, 0))
    matrices0[4 * levels : 8 * levels, :] = turned(four(0, 4))


def to_scalars(sources, target, sems):
    copies = [pltpu.make_async_copy(source, target.at[n], sems.at[n]) for n, source in enumerate(sources)]
    for copy in copies:
        copy.start()
    return copies


def first_spread(levels, count, *refs):
    messages, refs = refs[:count], refs[count:]
    (*refs, masks, tables, sems) = refs
    per_field = 8 * levels
    me, lat_start = lax.axis_index("lon"), 8 * lax.axis_index("lat")
    copies = to_scalars([message.at[pl.ds(per_field + 64, 8)] for message in messages], tables, sems)
    if len(refs) == 1:
        (acc,) = refs
        acc[...] = jnp.zeros_like(acc)
    else:
        before, acc, *out = refs
        acc[...] = before[...]
    stay, back, on = lane_masks()
    for n, mask in enumerate((stay, back, jnp.zeros_like(stay), on)):
        masks[n] = mask
    for copy in copies:
        copy.wait()
    for at, message in enumerate(messages):
        for i in range(8):
            first = tables[at, 1, i].astype(jnp.int32) - lat_start + LOW
            tau = tables[at, 3, i].astype(jnp.int32)
            delta = (tau - me) & 3
            block = (tau + jnp.where(delta == 1, 7, jnp.where(delta == 3, 1, 0))) & 7
            weights = message[pl.ds(per_field + i, 8, stride=8), :]
            terms = masked(products(weights), masks[delta], range(NODES))
            sources = [rolled(message[pl.ds(8 * kk + i, 8, stride=8), :]) for kk in range(0, levels, 8)]
            add_terms(sources, terms, acc, (block // 4) * 15 + first)
    if len(refs) < 4:
        return
    even = even_band()

    def write(to, part_row, rows):
        for h in range(2):
            value = acc[h * 15 + part_row : h * 15 + part_row + rows]
            to[h * 8 * levels : (h * 8 + rows) * levels, :] = value.reshape(rows * levels, 128)

    for to, is_upper in zip(out, (even == 1, even == 0)):

        @pl.when(is_upper)
        def _(to=to):
            write(to, 7, 8)

        @pl.when(~is_upper)
        def _(to=to):
            write(to, 0, 6)


def vertical(matrix, column):
    high = column.astype(jnp.bfloat16)
    low = (column - high.astype(jnp.float32)).astype(jnp.bfloat16)
    return jnp.dot(matrix, jnp.concatenate([high, high, low, low], axis=0), preferred_element_type=jnp.float32)


def finish_rows(levels, upper, part, received, matrices, state, at):
    band = lax.axis_index("lat")
    base = 8 * upper
    sender = jnp.where(upper == 1, band < lax.axis_size("lat") - 1, band > 0)
    for j in range(8):
        halves = []
        for h in range(2):
            sent = received[pl.ds(pl.multiple_of((h * 8 + j - upper) * levels, levels) if j else h * 8 * levels, levels), :]
            sent = jnp.where(sender, sent, 0.0)
            if j == 0:
                value = jnp.where(upper == 1, part[h * 15 + 7], sent)
            else:
                value = part[h * 15 + base + j - 1] + sent
            if j == 7:
                value = jnp.where(upper == 1, 0.0, value)
            halves.append(value)
        matrix = matrices[pl.ds(pl.multiple_of((base + j) * levels, levels), levels), :]
        result = vertical(matrix, jnp.concatenate(halves, axis=1))
        state[at + j] = result[:, :128]
        state[at + 8 + j] = result[:, 128:]


def spread_rows(levels, upper, own_pack, y_pack, state, at, tables, acc):
    me, band = lax.axis_index("lon"), lax.axis_index("lat")
    lat_start, at_start, at_end = 8 * band, band == 0, band == lax.axis_size("lat") - 1
    slot = me // 4
    stay, back, on = lane_masks()
    for j in range(8):
        n = 8 * upper + j
        there = (n < 15) & (~at_start | (n >= 4) if j < 4 else ~at_end | (n < 12))
        rows = pl.ds(pl.multiple_of(8 * n, 8), 8)
        for h in range(2):
            mine = slot == h
            tau = jnp.where(there, jnp.where(mine, tables[0, 2, n], tables[1, 2, n]).astype(jnp.int32), 0)
            first = jnp.where(mine, tables[0, 0, n], tables[1, 0, n]).astype(jnp.int32) - lat_start + 7
            first = jnp.where(there, first, 7)
            prods = products(jnp.where(there, jnp.where(mine, own_pack[rows, :], y_pack[rows, :]), 0.0))
            sources = [rolled(state[at + h * 8 + j, kk : kk + 8, :]) for kk in range(0, levels, 8)]
            add_terms(sources, masked(prods, stay, range(NODES)), acc, (tau ^ me) * 22 + first)
            add_terms(sources, masked(prods, back, (0,)), acc, (((tau + 7) & 7) ^ me) * 22 + first)
            add_terms(sources, masked(prods, on, (2, 3)), acc, (((tau + 1) & 7) ^ me) * 22 + first)


def second_spread(levels, part, r1, r2, own_pack, y_pack, matrices, *refs):
    outs, (state, tables, sems, acc) = refs[:8], refs[8:]
    copies = to_scalars([pack.at[pl.ds(120, 8)] for pack in (own_pack, y_pack)], tables, sems)
    even = even_band()
    finish_rows(levels, even, part, r1, matrices, state, 0)
    finish_rows(levels, 1 - even, part, r2, matrices, state, 16)
    for q in range(8):
        acc[q * 22 + 7 : q * 22 + 15] = jnp.zeros((8, levels, 128), jnp.float32)
    for copy in copies:
        copy.wait()
    spread_rows(levels, even, own_pack, y_pack, state, 0, tables, acc)
    spread_rows(levels, 1 - even, own_pack, y_pack, state, 16, tables, acc)
    for q, out in enumerate(outs):
        out[...] = acc[q * 22 + 7 : q * 22 + 15].reshape(8 * levels, 128)


def finish(levels, own, diagonal, across, up, pair, matrices, out):
    field = lax.axis_index("lon") // 4
    for i in range(8):
        rows = slice(i * levels, (i + 1) * levels)
        mine = own[rows, :] + pair[rows, :] + across[rows, :]
        other = up[rows, :] + diagonal[rows, :]
        result = vertical(matrices[rows, :], jnp.concatenate([mine, other], axis=1))
        for kk in range(0, levels, 8):
            out[pl.ds((field * levels + kk) * 8 + i, 8, stride=8), :] = result[kk : kk + 8, :128]
            out[pl.ds(((1 - field) * levels + kk) * 8 + i, 8, stride=8), :] = result[kk : kk + 8, 128:]


def swap_lon(value, bits):
    return lax.ppermute(value, "lon", [(i, i ^ bits) for i in range(RING)])


def swap_lat(value, odd):
    count = lax.axis_size("lat")
    pairs = [(i, i + 1) for i in range(odd, count - 1, 2)]
    partner = {a: b for pair in pairs for a, b in (pair, pair[::-1])}
    moves = [(i * RING + j, partner[i] * RING + j if i in partner else i * RING + (j ^ 1)) for i in range(count) for j in range(RING)]
    return lax.ppermute(value, ("lat", "lon"), moves)


def ring_body(adjoint_in, lat_weights, lon_weights, depart_rows, depart_blocks, vertical_inverse):
    fields, levels, lat_rows, points = adjoint_in.shape
    per_field = 8 * levels
    size = adjoint_in.size
    message = per_field + 64 + 8
    side = 32 + levels + 8
    adjoint = adjoint_in.reshape(-1, points)
    lat_w, lon_w = lat_weights.reshape(-1, points), lon_weights.reshape(-1, points)
    shapes = [(n, points) for n in (message, message, side, side, 64, 64)] + [vertical_inverse.shape]
    arguments = depart_rows[:, :, 0], depart_blocks[:, :, 0], adjoint, lat_w, lon_w, vertical_inverse
    own, other, e1, e2, lat_w, lon_w, matrices = pl.pallas_call(
        functools.partial(assemble, levels),
        out_shape=[pltpu.VMEM(shape, jnp.float32) for shape in shapes],
        in_specs=[pl.BlockSpec(memory_space=pltpu.HBM)] * 6,
        out_specs=[pl.BlockSpec(memory_space=pltpu.VMEM)] * 7,
        scratch_shapes=[pltpu.VMEM((2, 2, 8), jnp.int32), pltpu.SemaphoreType.DMA((7,))],
        compiler_params=pltpu.CompilerParams(vmem_limit_bytes=VMEM_LIMIT),
    )(*(pltpu.with_memory_space_constraint(value, pltpu.HBM) for value in arguments))
    far = {2: swap_lon(own, 2), 4: swap_lon(other, 4), 6: swap_lon(other, 6)}
    tile = pl.BlockSpec((8, 128), lambda i: (message // 8 - 1, 0), memory_space=pltpu.VMEM)
    e1, e2 = swap_lat(e1, 0), swap_lat(e2, 1)
    partial = ((30, levels, 128), jnp.float32)

    def spread(those, *before, outs=()):
        count = len(those)
        scratch = [pltpu.VMEM((4, 8, 128), jnp.float32), pltpu.SMEM((count, 8, 128), jnp.float32)]
        return call(
            functools.partial(first_spread, levels, count),
            [partial, *outs],
            [vmem((message, 128))] * count + [vmem(partial[0], 3)] * len(before),
            scratch + [pltpu.SemaphoreType.DMA((count,))],
            4 * size,
            *those,
            *before,
        )

    (part,) = spread([own])
    far[4], part, e1 = lax.optimization_barrier((far[4], part, e1))
    far[6], e2 = lax.optimization_barrier((far[6], e2))
    (part,) = spread([far[4], far[6], far[2]], part)
    others = [swap_lon(value, 1) for value in (own, far[4], far[6], far[2])]
    part, m1, m2 = spread(others, part, outs=(16 * levels, 16 * levels))
    r1, r2 = swap_lat(m1, 0), swap_lat(m2, 1)
    pack, matrices1, matrices0 = call(
        functools.partial(rim_data, levels),
        [128, ((16 * levels, 128), jnp.bfloat16), ((8 * levels, 128), jnp.bfloat16)],
        [tile, vmem((64, 128)), vmem((64, 128)), vmem((side, 128)), vmem((side, 128))]
        + [vmem(vertical_inverse.shape, 4), vmem((8, levels, 128), 3)],
        [],
        size,
        own,
        lat_w,
        lon_w,
        e1,
        e2,
        matrices,
        part,
    )
    y_pack = swap_lon(pack, 4)
    pieces = call(
        functools.partial(second_spread, levels),
        [8 * levels] * 8,
        [vmem(partial[0], 3)] + [vmem((16 * levels, 128))] * 2 + [vmem((128, 128))] * 2 + [vmem((16 * levels, 128))],
        [
            pltpu.VMEM((32, levels, 128), jnp.float32),
            pltpu.SMEM((2, 8, 128), jnp.float32),
            pltpu.SemaphoreType.DMA((2,)),
            pltpu.VMEM((8 * 22, levels, 128), jnp.float32),
        ],
        16 * size,
        *(part, r1, r2, pack, y_pack, matrices1),
    )
    received = {}
    for bits in (6, 4, 2):
        received[bits] = swap_lon(pieces[bits] + swap_lon(pieces[bits + 1], 1), bits)
    pair = swap_lon(pieces[1], 1)
    (out,) = call(
        functools.partial(finish, levels),
        [fields * levels * 8],
        [vmem((8 * levels, 128))] * 6,
        [],
        size,
        pieces[0],
        received[6],
        received[2],
        received[4],
        pair,
        matrices0,
    )
    return out.reshape(adjoint_in.shape)


def solution(mesh):
    specs = (
        P(None, None, "lat", "lon"),
        P(None, None, "lat", "lon"),
        P(None, None, "lat", "lon"),
        P(None, "lat", "lon"),
        P(None, "lat", "lon"),
        P(None, "lat", None, None),
    )

    def whole(*args):
        fields, levels, rows, points = args[0].shape
        lat, lon = mesh.shape["lat"], mesh.shape["lon"]
        ring = (fields, lon, rows // lat, points // lon) == (2, RING, 8, 128) and levels % 8 == 0 and levels * 4 == 128
        body = ring_body if ring else plain_body
        return jax.shard_map(body, mesh=mesh, in_specs=specs, out_specs=specs[0], check_vma=False)(*args)

    return whole
```
